32 devices in a mesh: seq: 4 (over z), chan: 4 (over y, x), dp: 2 (over core).
Axes of the slice: x: 2, y: 2, z: 4, core: 2. Of those that a mesh axis runs over, the one named last changes fastest.
Arguments:
- query_proj: bfloat16 [2, 2048, 8192], P('dp', 'seq', 'chan'), may hold values from -6 to 6
- key_proj: bfloat16 [2, 2048, 8192], P('dp', 'seq', 'chan')
- value_proj: bfloat16 [2, 2048, 8192], P('dp', 'seq', 'chan')
- cotangent: bfloat16 [2, 2048, 8192], P('dp', 'seq', 'chan'), may hold values from -6 to 6
- long_filter: float32 [2048, 8192], P('seq', 'chan')
- skip_gain: float32 [8192], P('chan'), may hold values from -3 to 3
Outputs:
- output: bfloat16 [2, 2048, 8192], P('dp', 'seq', 'chan')
- grad_query: bfloat16 [2, 2048, 8192], P('dp', 'seq', 'chan')
- grad_key: bfloat16 [2, 2048, 8192], P('dp', 'seq', 'chan')
- grad_value: bfloat16 [2, 2048, 8192], P('dp', 'seq', 'chan')
- grad_filter: float32 [2048, 8192], P('seq', 'chan')
- grad_skip: float32 [8192], P('chan')
The draws below stay inside these ranges and needn't reach their ends.
All inputs are finite; a program needn't handle non-finite values.
Results may differ from the reference program's by a relative error of at most 0.0095.
Values may be sent and summed in bfloat16 or wider, within the bound.
A program may use at most 128 MiB of HBM per device.

```python
import math
import jax
import jax.numpy as jnp
from jax import lax

D = 8192
L = 2048
B = 2


def draw_long_filter(key, part):
    unit = jax.random.uniform(jax.random.fold_in(key, 11), (D,), jnp.float32)
    lowest = math.log(0.5 / L)
    highest = math.log(1.0 / 32.0)
    positions = jnp.arange(L).astype(jnp.float32)
    rate = jnp.exp(lowest + unit * (highest - lowest))
    noise = jax.random.normal(jax.random.fold_in(key, 13), (L, D), jnp.float32)
    envelope = jnp.sqrt(2.0 * rate)[None, :] * jnp.exp(-rate[None, :] * positions[:, None])
    tail_height = jax.random.uniform(jax.random.fold_in(key, 14), (D,), jnp.float32, 0.8, 1.2) * (0.0077 / math.sqrt(L))
    tail = tail_height[None, :] * jnp.exp(-positions[:, None] / float(L))
    return (noise * envelope + tail).astype(jnp.float32)


def shared_offset(key):
    base = jax.random.fold_in(key, 21)
    amplitude = jax.random.uniform(jax.random.fold_in(base, 1), (B, 1, D), jnp.float32, 0.6, 1.2)
    flip = jax.random.uniform(jax.random.fold_in(base, 2), (B, 1, D), jnp.float32)
    sign_part = jnp.where(flip < 0.5, -1.0, 1.0).astype(jnp.float32)
    phase = jax.random.uniform(jax.random.fold_in(base, 3), (B, 1, D), jnp.float32, -math.pi, math.pi)
    positions = jnp.arange(L).astype(jnp.float32)[None, :, None]
    return sign_part * amplitude * (0.8 + 0.4 * jnp.cos(2.0 * math.pi / L * positions + phase))


def branch_noise(key, salt):
    noise = jnp.clip(jax.random.normal(jax.random.fold_in(key, salt), (B, L, D), jnp.float32), -4.0, 4.0)
    return noise


def draw_key_proj(key, part):
    values = shared_offset(key) + branch_noise(key, 22)
    return jnp.clip(values, -6.0, 6.0).astype(jnp.bfloat16)


def draw_value_proj(key, part):
    values = shared_offset(key) + branch_noise(key, 23)
    return jnp.clip(values, -6.0, 6.0).astype(jnp.bfloat16)


def block_scale(stream_key, dims, shards, least, top_value):
    loudness = 1.0
    for dim, blocks in shards:
        steps = jax.random.uniform(jax.random.fold_in(jax.random.fold_in(stream_key, 6), dim), (blocks,), jnp.float32, least / len(shards), top_value / len(shards))
        loudness = loudness * jnp.repeat(jnp.exp(steps), dims[dim] // blocks).reshape((-1,) + (1,) * (len(dims) - 1 - dim))
    return loudness


def centred(own_key, dims, scale, reach, split=(), kind=jnp.bfloat16):
    entries = jax.random.normal(own_key, dims, jnp.float32) * scale
    if len(split) > 0:
        entries = block_scale(own_key, dims, split, -0.22, 0.18) * entries
    return jnp.clip(entries, min=-reach, max=reach).astype(kind)


def setup_inputs(seed: int = 0) -> dict:
    key_list = jax.random.split(jax.random.key(seed), 7)
    return {
        "query_proj": centred(key_list[0], (B, L, D), 1.0, 6.0, ((0, 2), (1, 4), (2, 4))),
        "key_proj": draw_key_proj(jax.random.fold_in(key_list[6], 71), 0),
        "value_proj": draw_value_proj(jax.random.fold_in(key_list[6], 71), 0),
        "cotangent": centred(key_list[3], (B, L, D), 1.0, 6.0, ((0, 2), (1, 4), (2, 4))),
        "long_filter": draw_long_filter(jax.random.fold_in(key_list[6], 71), 0),
        "skip_gain": centred(key_list[5], (D,), 0.5, 3.0, ((0, 4),), jnp.float32),
    }


def channel_block(items):
    query_blk, key_blk, value_blk, cot_blk, filter_blk, skip_blk = items
    full_size = 2 * L
    kernel = filter_blk.astype(jnp.float32)
    mixed = (key_blk.astype(jnp.float32) * value_blk.astype(jnp.float32)).astype(jnp.bfloat16)
    weighted = (cot_blk.astype(jnp.float32) * query_blk.astype(jnp.float32)).astype(jnp.bfloat16)
    mixed_wide = mixed.astype(jnp.float32)
    weighted_wide = weighted.astype(jnp.float32)
    mixed_spec = jnp.fft.rfft(mixed_wide, n=full_size, axis=1)
    weighted_spec = jnp.fft.rfft(weighted_wide, n=full_size, axis=1)
    kernel_spec = jnp.fft.rfft(kernel, n=full_size, axis=0)[None]
    conv_vals = jnp.fft.irfft(mixed_spec * kernel_spec, n=full_size, axis=1)[:, :L].astype(jnp.bfloat16)
    corr_vals = jnp.fft.irfft(jnp.conj(kernel_spec) * weighted_spec, n=full_size, axis=1)[:, :L].astype(jnp.bfloat16)
    signal = conv_vals.astype(jnp.float32) + skip_blk[None, None, :] * mixed_wide
    output = (query_blk.astype(jnp.float32) * signal).astype(jnp.bfloat16)
    grad_query = (cot_blk.astype(jnp.float32) * signal).astype(jnp.bfloat16)
    back = corr_vals.astype(jnp.float32) + skip_blk[None, None, :] * weighted_wide
    grad_key = (back * value_blk.astype(jnp.float32)).astype(jnp.bfloat16)
    grad_value = (back * key_blk.astype(jnp.float32)).astype(jnp.bfloat16)
    slope_spec = jnp.sum(jnp.conj(mixed_spec) * weighted_spec, axis=0)
    slope = jnp.fft.irfft(slope_spec, n=full_size, axis=0)[:L]
    factor = (B * L) ** -0.5
    grad_filt = factor * slope
    grad_gain = factor * jnp.sum(weighted_wide * mixed_wide, axis=(0, 1))
    return output, grad_query, grad_key, grad_value, grad_filt, grad_gain


def reference(query_proj, key_proj, value_proj, cotangent, long_filter, skip_gain):
    block_width = min(D, 512)
    block_count = D // block_width

    def stack_blocks(arr):
        return jnp.moveaxis(arr.reshape(B, L, block_count, block_width), 2, 0)

    items = (stack_blocks(query_proj), stack_blocks(key_proj), stack_blocks(value_proj), stack_blocks(cotangent),
             jnp.moveaxis(long_filter.reshape(L, block_count, block_width), 1, 0),
             skip_gain.reshape(block_count, block_width))
    results = lax.map(channel_block, items)

    def unstack_blocks(arr):
        return jnp.moveaxis(arr, 0, 2).reshape(B, L, D)

    output, grad_query, grad_key, grad_value, grad_filt, grad_gain = results
    return (unstack_blocks(output), unstack_blocks(grad_query), unstack_blocks(grad_key), unstack_blocks(grad_value),
            jnp.moveaxis(grad_filt, 0, 1).reshape(L, D), grad_gain.reshape(D))
```

```python
import functools
import math

import jax
import jax.numpy as jnp
import ml_dtypes
import numpy as np
from jax import lax
from jax.experimental import pallas as pl
from jax.experimental.pallas import tpu as pltpu
from jax.sharding import PartitionSpec as P

full_precision = lax.Precision.HIGHEST
MESH = pl.DeviceIdType.MESH
LANES = 128
INNER = 128
ROWS = 16


def transform_tables(seq_length):
    full_size = 2 * seq_length
    outer = full_size // INNER
    firsts = outer // 2
    kept = outer // 2 + 1
    k1 = np.arange(kept)
    n1 = np.arange(firsts)
    first = 2.0 * np.pi * (k1[:, None] * n1[None, :] % outer) / outer
    first_parts = np.stack([np.cos(first), -np.sin(first)], axis=1).reshape(2 * kept, firsts)
    enter = np.kron(first_parts, np.eye(ROWS))
    weight = np.where((k1 == 0) | (k1 == outer // 2), 1.0, 2.0) / full_size
    leave = np.kron((first_parts.reshape(kept, 2, firsts) * weight[:, None, None]).reshape(2 * kept, firsts).T, np.eye(ROWS))
    n2 = np.arange(INNER)
    k2 = np.arange(INNER)
    freq = k1[:, None, None] + outer * k2[None, :, None]
    angle = 2.0 * np.pi * (freq * n2[None, None, :] % full_size) / full_size
    cos, sin = np.cos(angle), np.sin(angle)
    middle = np.concatenate(
        [np.concatenate([cos, sin], axis=2), np.concatenate([-sin, cos], axis=2)], axis=1
    )
    back = np.transpose(middle, (0, 2, 1))
    return tuple(np.asarray(t).astype(ml_dtypes.bfloat16) for t in (enter, middle, back, leave))


def fused_kernel(
    seq_count, batch_count, factor,
    q_hbm, k_hbm, v_hbm, ct_hbm, taps_hbm, skip_ref, enter_ref, middle_ref, back_ref, leave_ref,
    out_hbm, gq_hbm, gk_hbm, gv_hbm, gf_hbm, gs_ref,
    acts, taps, stage, hstage, xrecv, hrecv, spec, res, sres, rrecv, srecv, gain,
    in_sem, out_sem, x_send, x_recv, h_send, h_recv, r_send, r_recv, s_send, s_recv, f_send, g_send, g_recv,
):
    z = lax.axis_index("seq")
    b = lax.axis_index("dp")
    groups = seq_count * batch_count
    me = z * batch_count + b
    block_count, rows = acts.shape[1], acts.shape[2]
    chunks = block_count // groups
    kept = middle_ref.shape[0]
    per_row = rows // INNER
    firsts = seq_count * per_row
    act_in = (q_hbm, k_hbm, v_hbm, ct_hbm)
    act_out = (out_hbm, gq_hbm, gk_hbm, gv_hbm)

    def partner(i):
        pz = lax.rem(z + 1 + i // batch_count, seq_count)
        pb = lax.rem(b + 1 + lax.rem(i, batch_count), batch_count)
        return pz, pb, pz * batch_count + pb

    def cols(blk):
        return pl.ds(pl.multiple_of(blk * LANES, LANES), LANES)

    def start_input(j, carry):
        c = j // groups
        _, _, idx = partner(lax.rem(j, groups))
        blk = c * groups + idx
        for a in range(4):
            pltpu.make_async_copy(
                act_in[a].at[0, :, cols(blk)], acts.at[a, blk], in_sem.at[a, blk]
            ).start()
        pltpu.make_async_copy(taps_hbm.at[:, cols(blk)], taps.at[blk], in_sem.at[4, blk]).start()
        return carry

    lax.fori_loop(0, block_count, start_input, 0)

    barrier = pltpu.get_barrier_semaphore()

    def greet(i, carry):
        pz, pb, _ = partner(i)
        pl.semaphore_signal(barrier, inc=1, device_id={"seq": pz, "dp": pb}, device_id_type=MESH)
        return carry

    lax.fori_loop(0, groups - 1, greet, 0)
    pl.semaphore_wait(barrier, groups - 1)

    def remote(src, dst, send, recv, pz, pb):
        return pltpu.make_async_remote_copy(
            src_ref=src, dst_ref=dst, send_sem=send, recv_sem=recv,
            device_id={"seq": pz, "dp": pb}, device_id_type=MESH,
        )

    def send_block(j, carry):
        c = j // groups
        pz, pb, idx = partner(lax.rem(j, groups))
        blk = c * groups + idx
        for a in range(4):
            pltpu.make_async_copy(
                act_in[a].at[0, :, cols(blk)], acts.at[a, blk], in_sem.at[a, blk]
            ).wait()
        pltpu.make_async_copy(taps_hbm.at[:, cols(blk)], taps.at[blk], in_sem.at[4, blk]).wait()
        mixed = (acts[1, blk].astype(jnp.float32) * acts[2, blk].astype(jnp.float32)).astype(jnp.bfloat16)
        weighted = (acts[3, blk].astype(jnp.float32) * acts[0, blk].astype(jnp.float32)).astype(jnp.bfloat16)
        stage[blk, 0] = mixed
        stage[blk, 1] = weighted
        gain[me, pl.ds(blk, 1), :] = jnp.sum(
            weighted.astype(jnp.float32) * mixed.astype(jnp.float32), axis=0, keepdims=True
        )

        @pl.when(idx != me)
        def _():
            remote(stage.at[blk], xrecv.at[c, me], x_send.at[blk], x_recv.at[c, me], pz, pb).start()

        @pl.when(idx == me)
        def _():
            pltpu.make_async_copy(stage.at[blk], xrecv.at[c, me], x_recv.at[c, me]).start()

        @pl.when(pb == b)
        def _():
            hstage[c, pz] = taps[blk].astype(jnp.bfloat16)

            @pl.when(pz != z)
            def _():
                remote(hstage.at[c, pz], hrecv.at[c, z], h_send.at[c, pz], h_recv.at[c, z], pz, b).start()

            @pl.when(pz == z)
            def _():
                pltpu.make_async_copy(hstage.at[c, pz], hrecv.at[c, z], h_recv.at[c, z]).start()

        return carry

    lax.fori_loop(0, block_count, send_block, 0)

    def send_gain(i, carry):
        pz, pb, idx = partner(i)
        remote(gain.at[me], gain.at[me], g_send.at[idx], g_recv.at[me], pz, pb).start()
        return carry

    lax.fori_loop(0, groups - 1, send_gain, 0)

    def arrived(ref, sem):
        pltpu.make_async_copy(ref, ref, sem).wait()

    def transform(c, carry):
        def wait_x(s, inner):
            arrived(xrecv.at[c, s], x_recv.at[c, s])
            return inner

        def wait_h(s, inner):
            arrived(hrecv.at[c, s], h_recv.at[c, s])
            return inner

        lax.fori_loop(0, groups, wait_x, 0)
        lax.fori_loop(0, seq_count, wait_h, 0)

        def enter(g, inner):
            def piece(ref):
                return jnp.concatenate(
                    [
                        ref(n1 // per_row, pl.ds(pl.multiple_of(n1 % per_row * INNER + g * ROWS, ROWS), ROWS))
                        for n1 in range(firsts)
                    ],
                    axis=0,
                )

            signals = []
            for a in range(2):
                for bb in range(batch_count):
                    signals.append(piece(lambda s, r, a=a, bb=bb: xrecv[c, s * batch_count + bb, a, r, :]))
            signals.append(piece(lambda s, r: hrecv[c, s, r, :]))
            stacked = jnp.concatenate(signals, axis=1)
            grid = jnp.dot(enter_ref[...], stacked, preferred_element_type=jnp.float32).astype(jnp.bfloat16)
            for k1 in range(kept):
                for part in range(2):
                    at = (2 * k1 + part) * ROWS
                    spec[k1, pl.ds(pl.multiple_of(part * INNER + g * ROWS, ROWS), ROWS), :] = grid[at : at + ROWS]
            return inner

        lax.fori_loop(0, INNER // ROWS, enter, 0)

        def middle(k1, inner):
            full = jnp.dot(middle_ref[k1], spec[k1], preferred_element_type=jnp.float32)
            real, imag = full[:INNER], full[INNER:]

            def take(i):
                return real[:, i * LANES : (i + 1) * LANES], imag[:, i * LANES : (i + 1) * LANES]

            hr, hi = take(2 * batch_count)
            out_real, out_imag = [], []
            for bb in range(batch_count):
                mr, mi = take(bb)
                out_real.append(mr * hr - mi * hi)
                out_imag.append(mr * hi + mi * hr)
            for bb in range(batch_count):
                wr, wi = take(batch_count + bb)
                out_real.append(hr * wr + hi * wi)
                out_imag.append(hr * wi - hi * wr)
            slope_real, slope_imag = 0.0, 0.0
            for bb in range(batch_count):
                mr, mi = take(bb)
                wr, wi = take(batch_count + bb)
                slope_real = slope_real + (mr * wr + mi * wi)
                slope_imag = slope_imag + (mr * wi - mi * wr)
            out_real.append(slope_real)
            out_imag.append(slope_imag)
            product = jnp.concatenate(
                [
                    jnp.concatenate([t.astype(jnp.bfloat16) for t in out_real], axis=1),
                    jnp.concatenate([t.astype(jnp.bfloat16) for t in out_imag], axis=1),
                ],
                axis=0,
            )
            spec[k1] = jnp.dot(back_ref[k1], product, preferred_element_type=jnp.float32).astype(jnp.bfloat16)
            return inner

        lax.fori_loop(0, kept, middle, 0)

        def leave(g, inner):
            stacked = jnp.concatenate(
                [
                    spec[k1, pl.ds(pl.multiple_of(part * INNER + g * ROWS, ROWS), ROWS), :]
                    for k1 in range(kept)
                    for part in range(2)
                ],
                axis=0,
            )
            grid = jnp.dot(leave_ref[...], stacked, preferred_element_type=jnp.float32).astype(jnp.bfloat16)
            for n1 in range(firsts):
                s = n1 // per_row
                r = pl.ds(pl.multiple_of(n1 % per_row * INNER + g * ROWS, ROWS), ROWS)
                part = grid[n1 * ROWS : (n1 + 1) * ROWS]
                for bb in range(batch_count):
                    res[c, s * batch_count + bb, 0, r, :] = part[:, bb * LANES : (bb + 1) * LANES]
                    at = batch_count + bb
                    res[c, s * batch_count + bb, 1, r, :] = part[:, at * LANES : (at + 1) * LANES]
                sres[c, s, r, :] = part[:, 2 * batch_count * LANES :]
            return inner

        lax.fori_loop(0, INNER // ROWS, leave, 0)

        mine = c * groups + me

        def send_result(i, inner):
            pz, pb, idx = partner(i)

            @pl.when(jnp.logical_and(pb == b, pz != z))
            def _():
                remote(sres.at[c, pz], srecv.at[mine], s_send.at[c, pz], s_recv.at[mine], pz, b).start()

            @pl.when(jnp.logical_and(pb == b, pz == z))
            def _():
                pltpu.make_async_copy(sres.at[c, pz], srecv.at[mine], s_recv.at[mine]).start()

            @pl.when(idx != me)
            def _():
                remote(res.at[c, idx], rrecv.at[mine], r_send.at[c, idx], r_recv.at[mine], pz, pb).start()

            @pl.when(idx == me)
            def _():
                pltpu.make_async_copy(res.at[c, idx], rrecv.at[mine], r_recv.at[mine]).start()

            return inner

        lax.fori_loop(0, groups, send_result, 0)
        return carry

    lax.fori_loop(0, chunks, transform, 0)

    def finish_chunk(c, carry):
        def finish_block(i, inner):
            pz = lax.rem(z + seq_count - i // batch_count, seq_count)
            pb = lax.rem(b + lax.rem(i, batch_count), batch_count)
            blk = c * groups + pz * batch_count + pb
            arrived(rrecv.at[blk], r_recv.at[blk])
            query = acts[0, blk].astype(jnp.float32)
            key = acts[1, blk].astype(jnp.float32)
            value = acts[2, blk].astype(jnp.float32)
            cot = acts[3, blk].astype(jnp.float32)
            skip = skip_ref[pl.ds(blk, 1), :]
            signal = rrecv[blk, 0].astype(jnp.float32) + skip * stage[blk, 0].astype(jnp.float32)
            back = rrecv[blk, 1].astype(jnp.float32) + skip * stage[blk, 1].astype(jnp.float32)
            acts[0, blk] = (query * signal).astype(jnp.bfloat16)
            acts[1, blk] = (cot * signal).astype(jnp.bfloat16)
            acts[2, blk] = (back * value).astype(jnp.bfloat16)
            acts[3, blk] = (back * key).astype(jnp.bfloat16)
            for a in range(4):
                pltpu.make_async_copy(
                    acts.at[a, blk], act_out[a].at[0, :, cols(blk)], out_sem.at[a, blk]
                ).start()
            arrived(srecv.at[blk], s_recv.at[blk])

            @pl.when(pb == b)
            def _():
                remote(srecv.at[blk], srecv.at[blk], f_send.at[c, pz], s_recv.at[blk], z, 1 - b).start()

            taps[blk] = factor * srecv[blk].astype(jnp.float32)
            pltpu.make_async_copy(taps.at[blk], gf_hbm.at[:, cols(blk)], out_sem.at[4, blk]).start()
            return inner

        lax.fori_loop(0, groups, finish_block, 0)
        return carry

    lax.fori_loop(0, chunks, finish_chunk, 0)

    def wait_gain(i, carry):
        _, _, idx = partner(i)
        arrived(gain.at[idx], g_recv.at[idx])
        return carry

    lax.fori_loop(0, groups - 1, wait_gain, 0)
    total = gain[0]
    for s in range(1, groups):
        total = total + gain[s]
    gs_ref[...] = factor * total

    def drain(j, carry):
        c = j // groups
        pz, pb, idx = partner(lax.rem(j, groups))
        blk = c * groups + idx
        for a in range(4):
            pltpu.make_async_copy(
                acts.at[a, blk], act_out[a].at[0, :, cols(blk)], out_sem.at[a, blk]
            ).wait()
        pltpu.make_async_copy(taps.at[blk], gf_hbm.at[:, cols(blk)], out_sem.at[4, blk]).wait()

        @pl.when(idx != me)
        def _():
            arrived(stage.at[blk], x_send.at[blk])
            arrived(res.at[c, idx], r_send.at[c, idx])

        @pl.when(jnp.logical_and(idx != me, c == 0))
        def _():
            arrived(gain.at[me], g_send.at[idx])

        @pl.when(pb == b)
        def _():
            arrived(srecv.at[blk], f_send.at[c, pz])

            @pl.when(pz != z)
            def _():
                arrived(hstage.at[c, pz], h_send.at[c, pz])
                arrived(sres.at[c, pz], s_send.at[c, pz])

        return carry

    lax.fori_loop(0, block_count, drain, 0)


def fused(query_proj, key_proj, value_proj, cotangent, long_filter, skip_gain):
    rows, width = query_proj.shape[1:]
    seq_count = lax.axis_size("seq")
    batch_count = lax.axis_size("dp")
    groups = seq_count * batch_count
    seq_length = seq_count * rows
    block_count = width // LANES
    chunks = block_count // groups
    factor = (batch_count * seq_length) ** (-0.5)
    tables = transform_tables(seq_length)
    kept = tables[1].shape[0]
    signals = 2 * batch_count + 1
    half = jnp.bfloat16
    dma = pltpu.SemaphoreType.DMA
    hbm = pl.BlockSpec(memory_space=pl.ANY)
    vmem = pl.BlockSpec(memory_space=pltpu.VMEM)
    flops = 2 * chunks * signals * LANES * (2 * tables[0].size * INNER // ROWS + 2 * tables[1].size)
    results = pl.pallas_call(
        functools.partial(fused_kernel, seq_count, batch_count, factor),
        out_shape=[jax.ShapeDtypeStruct((1, rows, width), half)] * 4
        + [
            jax.ShapeDtypeStruct((rows, width), jnp.float32),
            jax.ShapeDtypeStruct((block_count, LANES), jnp.float32),
        ],
        in_specs=[hbm] * 5 + [vmem] * 5,
        out_specs=[hbm] * 5 + [vmem],
        scratch_shapes=[
            pltpu.VMEM((4, block_count, rows, LANES), half),
            pltpu.VMEM((block_count, rows, LANES), jnp.float32),
            pltpu.VMEM((block_count, 2, rows, LANES), half),
            pltpu.VMEM((chunks, seq_count, rows, LANES), half),
            pltpu.VMEM((chunks, groups, 2, rows, LANES), half),
            pltpu.VMEM((chunks, seq_count, rows, LANES), half),
            pltpu.VMEM((kept, 2 * INNER, signals * LANES), half),
            pltpu.VMEM((chunks, groups, 2, rows, LANES), half),
            pltpu.VMEM((chunks, seq_count, rows, LANES), half),
            pltpu.VMEM((block_count, 2, rows, LANES), half),
            pltpu.VMEM((block_count, rows, LANES), half),
            pltpu.VMEM((groups, block_count, LANES), jnp.float32),
            dma((5, block_count)),
            dma((5, block_count)),
            dma((block_count,)),
            dma((chunks, groups)),
            dma((chunks, seq_count)),
            dma((chunks, seq_count)),
            dma((chunks, groups)),
            dma((block_count,)),
            dma((chunks, seq_count)),
            dma((block_count,)),
            dma((chunks, seq_count)),
            dma((groups,)),
            dma((groups,)),
        ],
        compiler_params=pltpu.CompilerParams(
            collective_id=0, has_side_effects=True, vmem_limit_bytes=60 * 1024 * 1024
        ),
        cost_estimate=pl.CostEstimate(
            flops=flops, bytes_accessed=24 * rows * width, transcendentals=0
        ),
    )(
        query_proj, key_proj, value_proj, cotangent, long_filter,
        skip_gain.reshape(block_count, LANES), *(jnp.asarray(t) for t in tables),
    )
    return tuple(results[:5]) + (results[5].reshape(width),)


def dft_tables(seq_length):
    full_size = 2 * seq_length
    inner_size = 128
    outer_size = full_size // inner_size
    half_size = outer_size // 2
    outer_index = jnp.arange(outer_size, dtype=jnp.int32)
    half_index = jnp.arange(half_size, dtype=jnp.int32)
    inner_index = jnp.arange(inner_size, dtype=jnp.int32)
    first_angle = (
        2.0
        * math.pi
        / outer_size
        * (outer_index[:, None] * half_index[None, :] % outer_size).astype(jnp.float32)
    )
    twist_angle = (
        2.0
        * math.pi
        / full_size
        * (outer_index[:, None] * inner_index[None, :] % full_size).astype(jnp.float32)
    )
    last_angle = (
        2.0
        * math.pi
        / inner_size
        * (inner_index[:, None] * inner_index[None, :] % inner_size).astype(jnp.float32)
    )
    return (
        jnp.cos(first_angle),
        jnp.sin(first_angle),
        jnp.cos(twist_angle),
        jnp.sin(twist_angle),
        jnp.cos(last_angle),
        jnp.sin(last_angle),
    )


def forward(signal, tables):
    cos_first, sin_first, cos_twist, sin_twist, cos_last, sin_last = tables
    half_size = cos_first.shape[1]
    signal_grid = signal.reshape(signal.shape[0], half_size, 128)
    real_first = jnp.einsum("kn,rnm->rkm", cos_first, signal_grid, precision=full_precision)
    imag_first = -jnp.einsum("kn,rnm->rkm", sin_first, signal_grid, precision=full_precision)
    real_twist = real_first * cos_twist + imag_first * sin_twist
    imag_twist = imag_first * cos_twist - real_first * sin_twist
    real_last = jnp.einsum(
        "rkm,mj->rkj", real_twist, cos_last, precision=full_precision
    ) + jnp.einsum("rkm,mj->rkj", imag_twist, sin_last, precision=full_precision)
    imag_last = jnp.einsum(
        "rkm,mj->rkj", imag_twist, cos_last, precision=full_precision
    ) - jnp.einsum("rkm,mj->rkj", real_twist, sin_last, precision=full_precision)
    return (real_last, imag_last)


def inverse(real_part, imag_part, tables):
    cos_first, sin_first, cos_twist, sin_twist, cos_last, sin_last = tables
    half_size = cos_first.shape[1]
    row_total = real_part.shape[0]
    real_inner = jnp.einsum(
        "rkj,jm->rkm", real_part, cos_last, precision=full_precision
    ) - jnp.einsum("rkj,jm->rkm", imag_part, sin_last, precision=full_precision)
    imag_inner = jnp.einsum(
        "rkj,jm->rkm", imag_part, cos_last, precision=full_precision
    ) + jnp.einsum("rkj,jm->rkm", real_part, sin_last, precision=full_precision)
    real_twist = real_inner * cos_twist - imag_inner * sin_twist
    imag_twist = imag_inner * cos_twist + real_inner * sin_twist
    result = jnp.einsum(
        "kn,rkm->rnm", cos_first, real_twist, precision=full_precision
    ) - jnp.einsum("kn,rkm->rnm", sin_first, imag_twist, precision=full_precision)
    return (result / (2.0 * half_size * 128)).reshape(row_total, half_size * 128)


def filter_block(items, tables):
    mixed_blk, weighted_blk, kernel = items
    batches, chan_width, seq_length = mixed_blk.shape
    row_count = batches * chan_width
    mixed_wide = mixed_blk.astype(jnp.float32)
    weighted_wide = weighted_blk.astype(jnp.float32)
    stacked = jnp.concatenate(
        [
            mixed_wide.reshape(row_count, seq_length),
            weighted_wide.reshape(row_count, seq_length),
            kernel,
        ],
        axis=0,
    )
    real_spec, imag_spec = forward(stacked, tables)
    grid_shape = real_spec.shape[1:]
    mixed_real = real_spec[:row_count].reshape((batches, chan_width) + grid_shape)
    mixed_imag = imag_spec[:row_count].reshape((batches, chan_width) + grid_shape)
    weighted_real = real_spec[row_count : 2 * row_count].reshape((batches, chan_width) + grid_shape)
    weighted_imag = imag_spec[row_count : 2 * row_count].reshape((batches, chan_width) + grid_shape)
    kernel_real = real_spec[2 * row_count :][None]
    kernel_imag = imag_spec[2 * row_count :][None]
    conv_real = mixed_real * kernel_real - mixed_imag * kernel_imag
    conv_imag = mixed_real * kernel_imag + mixed_imag * kernel_real
    corr_real = kernel_real * weighted_real + kernel_imag * weighted_imag
    corr_imag = kernel_real * weighted_imag - kernel_imag * weighted_real
    slope_real = jnp.sum(mixed_real * weighted_real + mixed_imag * weighted_imag, axis=0)
    slope_imag = jnp.sum(mixed_real * weighted_imag - mixed_imag * weighted_real, axis=0)
    spec_real = jnp.concatenate(
        [
            conv_real.reshape((row_count,) + grid_shape),
            corr_real.reshape((row_count,) + grid_shape),
            slope_real,
        ],
        axis=0,
    )
    spec_imag = jnp.concatenate(
        [
            conv_imag.reshape((row_count,) + grid_shape),
            corr_imag.reshape((row_count,) + grid_shape),
            slope_imag,
        ],
        axis=0,
    )
    result = inverse(spec_real, spec_imag, tables)
    conv_vals = result[:row_count].reshape(batches, chan_width, seq_length).astype(jnp.bfloat16)
    corr_vals = (
        result[row_count : 2 * row_count]
        .reshape(batches, chan_width, seq_length)
        .astype(jnp.bfloat16)
    )
    slope = result[2 * row_count :]
    return (conv_vals, corr_vals, slope)


def run_blocks(mixed_rows, weighted_rows, filter_part):
    batches, part_width, seq_length = mixed_rows.shape
    block_width = min(part_width, 8)
    block_count = part_width // block_width
    tables = dft_tables(seq_length)

    def stack_rows(arr):
        return jnp.moveaxis(arr.reshape(batches, block_count, block_width, seq_length), 1, 0)

    def unstack_rows(arr):
        return jnp.moveaxis(arr, 0, 1).reshape(batches, part_width, seq_length)

    def one_block(items):
        return filter_block(items, tables)

    items = (
        stack_rows(mixed_rows),
        stack_rows(weighted_rows),
        filter_part.reshape(block_count, block_width, seq_length),
    )
    conv_vals, corr_vals, slope = lax.map(one_block, items)
    return (unstack_rows(conv_vals), unstack_rows(corr_vals), slope.reshape(part_width, seq_length))


def on_device(query_proj, key_proj, value_proj, cotangent, long_filter, skip_gain):
    share = query_proj.shape[2] // (lax.axis_size("seq") * lax.axis_size("dp"))
    if share % LANES == 0 and query_proj.shape[1] % INNER == 0 and lax.axis_size("dp") == 2:
        return fused(query_proj, key_proj, value_proj, cotangent, long_filter, skip_gain)
    return spread(query_proj, key_proj, value_proj, cotangent, long_filter, skip_gain)


def spread(query_proj, key_proj, value_proj, cotangent, long_filter, skip_gain):
    query_rows = query_proj[0].astype(jnp.float32)
    key_rows = key_proj[0].astype(jnp.float32)
    value_rows = value_proj[0].astype(jnp.float32)
    cot_rows = cotangent[0].astype(jnp.float32)
    local_length = query_proj.shape[1]
    chan_width = query_proj.shape[2]
    seq_count = lax.axis_size("seq")
    batch_count = lax.axis_size("dp")
    factor = (batch_count * seq_count * local_length) ** (-0.5)
    mixed = (key_rows * value_rows).astype(jnp.bfloat16)
    weighted = (cot_rows * query_rows).astype(jnp.bfloat16)
    mixed_wide = mixed.astype(jnp.float32)
    weighted_wide = weighted.astype(jnp.float32)
    gain_term = factor * jnp.sum(weighted_wide * mixed_wide, axis=0)
    grad_skip = lax.psum(gain_term, ("seq", "dp"))
    filter_share = lax.all_to_all(long_filter.T, "seq", split_axis=0, concat_axis=1, tiled=True)
    groups = seq_count * batch_count
    share_width = chan_width // groups
    mixed_cols, weighted_cols = (
        lax.all_to_all(mixed.T, ("seq", "dp"), split_axis=0, concat_axis=1, tiled=True),
        lax.all_to_all(weighted.T, ("seq", "dp"), split_axis=0, concat_axis=1, tiled=True),
    )

    def to_sequences(arr):
        arr = arr.reshape(share_width, seq_count, batch_count, local_length)
        return jnp.transpose(arr, (2, 0, 1, 3)).reshape(
            batch_count, share_width, seq_count * local_length
        )

    def to_pieces(arr):
        arr = arr.reshape(batch_count, share_width, seq_count, local_length)
        return jnp.transpose(arr, (1, 2, 0, 3)).reshape(share_width, groups * local_length)

    filter_part = lax.dynamic_slice_in_dim(
        filter_share, lax.axis_index("dp") * share_width, share_width, 0
    )
    conv_vals, corr_vals, slope = run_blocks(
        to_sequences(mixed_cols), to_sequences(weighted_cols), filter_part
    )
    conv_back, corr_back = (
        lax.all_to_all(
            to_pieces(conv_vals), ("seq", "dp"), split_axis=1, concat_axis=0, tiled=True
        ),
        lax.all_to_all(
            to_pieces(corr_vals), ("seq", "dp"), split_axis=1, concat_axis=0, tiled=True
        ),
    )
    slope_share = lax.all_gather(slope, "dp", axis=0, tiled=True)
    slope_rows = lax.all_to_all(slope_share, "seq", split_axis=1, concat_axis=0, tiled=True)
    grad_filter = factor * slope_rows.T
    conv_rows = conv_back.T.astype(jnp.float32)
    corr_rows = corr_back.T.astype(jnp.float32)
    signal = conv_rows + skip_gain[None, :] * mixed_wide
    output = (query_rows * signal).astype(jnp.bfloat16)
    grad_query = (cot_rows * signal).astype(jnp.bfloat16)
    back = corr_rows + skip_gain[None, :] * weighted_wide
    grad_key = (back * value_rows).astype(jnp.bfloat16)
    grad_value = (back * key_rows).astype(jnp.bfloat16)
    return (
        output[None],
        grad_query[None],
        grad_key[None],
        grad_value[None],
        grad_filter,
        grad_skip,
    )


def solution(mesh):
    return jax.shard_map(
        on_device,
        mesh=mesh,
        in_specs=(
            P("dp", "seq", "chan"),
            P("dp", "seq", "chan"),
            P("dp", "seq", "chan"),
            P("dp", "seq", "chan"),
            P("seq", "chan"),
            P("chan"),
        ),
        out_specs=(
            P("dp", "seq", "chan"),
            P("dp", "seq", "chan"),
            P("dp", "seq", "chan"),
            P("dp", "seq", "chan"),
            P("seq", "chan"),
            P("chan"),
        ),
        check_vma=False,
    )
```

```python
import functools
import math

import jax
import jax.numpy as jnp
import ml_dtypes
import numpy as np
from jax import lax
from jax.experimental import pallas as pl
from jax.experimental.pallas import tpu as pltpu
from jax.sharding import PartitionSpec as P

full_precision = lax.Precision.HIGHEST
MESH = pl.DeviceIdType.MESH
LANES = 128
INNER = 128
ROWS = 16


def transform_tables(seq_length):
    full_size = 2 * seq_length
    outer = full_size // INNER
    firsts = outer // 2
    kept = outer // 2 + 1
    k1 = np.arange(kept)
    n1 = np.arange(firsts)
    first = 2.0 * np.pi * (k1[:, None] * n1[None, :] % outer) / outer
    first_parts = np.stack([np.cos(first), -np.sin(first)], axis=1).reshape(2 * kept, firsts)
    enter = np.kron(first_parts, np.eye(ROWS))
    weight = np.where((k1 == 0) | (k1 == outer // 2), 1.0, 2.0) / full_size
    leave = np.kron((first_parts.reshape(kept, 2, firsts) * weight[:, None, None]).reshape(2 * kept, firsts).T, np.eye(ROWS))
    n2 = np.arange(INNER)
    k2 = np.arange(INNER)
    freq = k1[:, None, None] + outer * k2[None, :, None]
    angle = 2.0 * np.pi * (freq * n2[None, None, :] % full_size) / full_size
    cos, sin = np.cos(angle), np.sin(angle)
    middle = np.concatenate(
        [np.concatenate([cos, sin], axis=2), np.concatenate([-sin, cos], axis=2)], axis=1
    )
    back = np.transpose(middle, (0, 2, 1))
    return tuple(np.asarray(t).astype(ml_dtypes.bfloat16) for t in (enter, middle, back, leave))


def fused_kernel(
    factor,
    q_hbm, k_hbm, v_hbm, ct_hbm, taps_hbm, skip_ref, enter_ref, middle_ref, back_ref, leave_ref, enter_low_ref, leave_low_ref,
    out_hbm, gq_hbm, gk_hbm, gv_hbm, gf_hbm, gs_ref,
    acts, taps, stage, hstage, xs, ws, hs, cross, scross, spec, ys, cs, ss, gain,
    in_sem, out_sem, x_send, x2_send, w_send, h_send, h2_send, f_send, y_send, c_send, s_send, n_send, g_send,
    x_recv, w_recv, h_recv, cross_recv, scross_recv, y_recv, c_recv, s_recv, g_recv,
):
    z = lax.axis_index("seq")
    b = lax.axis_index("dp")
    seq_count, batch_count = 4, 2
    groups = seq_count * batch_count
    me = z * batch_count + b
    block_count, rows = acts.shape[1], acts.shape[2]
    steps = block_count // batch_count
    per_row = rows // INNER
    act_in = (q_hbm, k_hbm, v_hbm, ct_hbm)
    act_out = (out_hbm, gq_hbm, gk_hbm, gv_hbm)

    def partner(i):
        pz = lax.rem(z + 1 + i // batch_count, seq_count)
        pb = lax.rem(b + 1 + lax.rem(i, batch_count), batch_count)
        return pz, pb, pz * batch_count + pb

    def cols(blk):
        return pl.ds(pl.multiple_of(blk * LANES, LANES), LANES)

    def upper_owner(k):
        return 3 - jnp.minimum(lax.rem(k, 4), 1)

    def input_copies(blk):
        found = [
            pltpu.make_async_copy(act_in[a].at[0, :, cols(blk)], acts.at[a, blk], in_sem.at[a, blk])
            for a in range(4)
        ]
        found.append(pltpu.make_async_copy(taps_hbm.at[:, cols(blk)], taps.at[blk], in_sem.at[4, blk]))
        return found

    def output_copies(blk):
        found = [
            pltpu.make_async_copy(acts.at[a, blk], act_out[a].at[0, :, cols(blk)], out_sem.at[a, blk])
            for a in range(4)
        ]
        found.append(pltpu.make_async_copy(taps.at[blk], gf_hbm.at[:, cols(blk)], out_sem.at[4, blk]))
        return found

    def start_input(blk, carry):
        for copy in input_copies(blk):
            copy.start()
        return carry

    lax.fori_loop(0, block_count, start_input, 0)

    barrier = pltpu.get_barrier_semaphore()

    def greet(i, carry):
        pz, pb, _ = partner(i)
        pl.semaphore_signal(barrier, inc=1, device_id={"seq": pz, "dp": pb}, device_id_type=MESH)
        return carry

    lax.fori_loop(0, groups - 1, greet, 0)
    pl.semaphore_wait(barrier, groups - 1)

    def remote(src, dst, send, recv, pz, pb):
        return pltpu.make_async_remote_copy(
            src_ref=src, dst_ref=dst, send_sem=send, recv_sem=recv,
            device_id={"seq": pz, "dp": pb}, device_id_type=MESH,
        )

    def arrived(ref, sem):
        pltpu.make_async_copy(ref, ref, sem).wait()

    def move(src, dst, send, recv, pz, pb):
        here = jnp.logical_and(pz == z, pb == b)

        @pl.when(here)
        def _():
            pltpu.make_async_copy(src, dst, recv).start()

        @pl.when(jnp.logical_not(here))
        def _():
            remote(src, dst, send, recv, pz, pb).start()

    def settle(src, dst, send, recv, pz, pb):
        @pl.when(jnp.logical_not(jnp.logical_and(pz == z, pb == b)))
        def _():
            arrived(src, send)

    def give_inputs(blk, act):
        k = blk // batch_count
        pb = lax.rem(blk, batch_count)
        owner = upper_owner(k)
        target = jnp.where(z < 2, 1, owner)
        slot = lax.rem(z, 2) * batch_count + b
        act(stage.at[blk, 0], xs.at[k, me], x_send.at[blk], x_recv.at[k, me], target, pb)

        @pl.when(pb == b)
        def _():
            act(hstage.at[k], hs.at[k, z], h_send.at[k], h_recv.at[k, z], target, b)

        @pl.when(z == 1)
        def _():
            act(stage.at[blk, 0], xs.at[k, me], x2_send.at[blk], x_recv.at[k, me], owner, pb)

            @pl.when(pb == b)
            def _():
                act(hstage.at[k], hs.at[k, z], h2_send.at[k], h_recv.at[k, z], owner, b)

        act(stage.at[blk, 1], ws.at[k, slot], w_send.at[blk], w_recv.at[k, slot], target, pb)

    def forward_low(k, act):
        owner = upper_owner(k)
        for bb in range(batch_count):
            act(xs.at[k, bb], xs.at[k, bb], f_send.at[k, bb], x_recv.at[k, bb], owner, b)
        act(hs.at[k, 0], hs.at[k, 0], f_send.at[k, 2], h_recv.at[k, 0], owner, b)

    def give_upper(k, act):
        blk = k * batch_count + b
        for zz in range(2):
            for bb in range(batch_count):
                at = zz * batch_count + bb
                act(xs.at[k, at], cross.at[k, at], c_send.at[k, at], cross_recv.at[k, at], 1, b)
            act(hs.at[k, zz], scross.at[k, zz], s_send.at[k, zz], scross_recv.at[k, zz], 1, b)
        for zz in range(2, 4):
            for bb in range(batch_count):
                at = zz * batch_count + bb
                low = at - 2 * batch_count
                act(ws.at[k, low], ys.at[blk], y_send.at[k, low], y_recv.at[blk], zz, bb)
                act(xs.at[k, at], cs.at[blk], c_send.at[k, at], c_recv.at[blk], zz, bb)
            act(hs.at[k, zz], ss.at[blk], s_send.at[k, zz], s_recv.at[blk], zz, b)

    def give_low_conv(k, act):
        blk = k * batch_count + b
        for zz in range(2):
            for bb in range(batch_count):
                at = zz * batch_count + bb
                act(ws.at[k, at], ys.at[blk], y_send.at[k, at], y_recv.at[blk], zz, bb)

    def give_low_corr(k, act):
        blk = k * batch_count + b
        for zz in range(2):
            for bb in range(batch_count):
                at = zz * batch_count + bb
                act(xs.at[k, 4 + at], cs.at[blk], c_send.at[k, at], c_recv.at[blk], zz, bb)
            act(hs.at[k, 2 + zz], ss.at[blk], s_send.at[k, zz], s_recv.at[blk], zz, b)

    def send_block(blk, carry):
        for copy in input_copies(blk):
            copy.wait()
        mixed = (acts[1, blk].astype(jnp.float32) * acts[2, blk].astype(jnp.float32)).astype(jnp.bfloat16)
        weighted = (acts[3, blk].astype(jnp.float32) * acts[0, blk].astype(jnp.float32)).astype(jnp.bfloat16)
        stage[blk, 0] = mixed
        stage[blk, 1] = weighted
        gain[me, pl.ds(blk, 1), :] = jnp.sum(
            weighted.astype(jnp.float32) * mixed.astype(jnp.float32), axis=0, keepdims=True
        )

        @pl.when(lax.rem(blk, batch_count) == b)
        def _():
            hstage[blk // batch_count] = taps[blk].astype(jnp.bfloat16)

        give_inputs(blk, move)
        return carry

    lax.fori_loop(0, block_count, send_block, 0)

    def send_gain(i, carry):
        pz, pb, idx = partner(i)
        remote(gain.at[me], gain.at[me], g_send.at[idx], g_recv.at[me], pz, pb).start()
        return carry

    lax.fori_loop(0, groups - 1, send_gain, 0)

    def transform(k, low):
        kept = (middle_ref.shape[0] + 1) // 2 if low else middle_ref.shape[0]
        firsts = (2 if low else 4) * per_row
        enter_table = enter_low_ref if low else enter_ref
        leave_table = leave_low_ref if low else leave_ref
        scale = 2 if low else 1

        def enter(g, inner):
            def piece(ref):
                return jnp.concatenate(
                    [
                        ref(n1 // per_row, pl.ds(pl.multiple_of(n1 % per_row * INNER + g * ROWS, ROWS), ROWS))
                        for n1 in range(firsts)
                    ],
                    axis=0,
                )

            def weighted_rows(s, r, bb):
                if low:
                    return ws[k, s * batch_count + bb, r, :]
                if s < 2:
                    return jnp.zeros((ROWS, LANES), jnp.bfloat16)
                return ws[k, (s - 2) * batch_count + bb, r, :]

            signals = [
                piece(lambda s, r, bb=bb: xs[k, s * batch_count + bb, r, :]) for bb in range(batch_count)
            ]
            signals += [piece(lambda s, r, bb=bb: weighted_rows(s, r, bb)) for bb in range(batch_count)]
            signals.append(piece(lambda s, r: hs[k, s, r, :]))
            stacked = jnp.concatenate(signals, axis=1)
            grid = jnp.dot(enter_table[...], stacked, preferred_element_type=jnp.float32).astype(jnp.bfloat16)
            for k1 in range(kept):
                for part in range(2):
                    at = (2 * k1 + part) * ROWS
                    spec[k1, pl.ds(pl.multiple_of(part * INNER + g * ROWS, ROWS), ROWS), :] = grid[at : at + ROWS]
            return inner

        lax.fori_loop(0, INNER // ROWS, enter, 0)

        def middle(k1, inner):
            full = jnp.dot(middle_ref[scale * k1], spec[k1], preferred_element_type=jnp.float32)
            real, imag = full[:INNER], full[INNER:]

            def take(i):
                return real[:, i * LANES : (i + 1) * LANES], imag[:, i * LANES : (i + 1) * LANES]

            hr, hi = take(2 * batch_count)
            out_real, out_imag = [], []
            for bb in range(batch_count):
                mr, mi = take(bb)
                out_real.append(mr * hr - mi * hi)
                out_imag.append(mr * hi + mi * hr)
            for bb in range(batch_count):
                wr, wi = take(batch_count + bb)
                out_real.append(hr * wr + hi * wi)
                out_imag.append(hr * wi - hi * wr)
            slope_real, slope_imag = 0.0, 0.0
            for bb in range(batch_count):
                mr, mi = take(bb)
                wr, wi = take(batch_count + bb)
                slope_real = slope_real + (mr * wr + mi * wi)
                slope_imag = slope_imag + (mr * wi - mi * wr)
            out_real.append(slope_real)
            out_imag.append(slope_imag)
            product = jnp.concatenate(
                [
                    jnp.concatenate([t.astype(jnp.bfloat16) for t in out_real], axis=1),
                    jnp.concatenate([t.astype(jnp.bfloat16) for t in out_imag], axis=1),
                ],
                axis=0,
            )
            spec[k1] = jnp.dot(back_ref[scale * k1], product, preferred_element_type=jnp.float32).astype(jnp.bfloat16)
            return inner

        lax.fori_loop(0, kept, middle, 0)

        def leave(g, inner):
            stacked = jnp.concatenate(
                [
                    spec[k1, pl.ds(pl.multiple_of(part * INNER + g * ROWS, ROWS), ROWS), :]
                    for k1 in range(kept)
                    for part in range(2)
                ],
                axis=0,
            )
            grid = jnp.dot(leave_table[...], stacked, preferred_element_type=jnp.float32).astype(jnp.bfloat16)
            for n1 in range(firsts):
                s = n1 // per_row
                r = pl.ds(pl.multiple_of(n1 % per_row * INNER + g * ROWS, ROWS), ROWS)
                part = grid[n1 * ROWS : (n1 + 1) * ROWS]
                for bb in range(batch_count):
                    if low:
                        ws[k, s * batch_count + bb, r, :] = part[:, bb * LANES : (bb + 1) * LANES]
                    elif s >= 2:
                        ws[k, (s - 2) * batch_count + bb, r, :] = part[:, bb * LANES : (bb + 1) * LANES]
                    at = batch_count + bb
                    to = s * batch_count + bb + (4 if low else 0)
                    xs[k, to, r, :] = part[:, at * LANES : (at + 1) * LANES]
                hs[k, s + (2 if low else 0), r, :] = part[:, 2 * batch_count * LANES :]
            return inner

        lax.fori_loop(0, INNER // ROWS, leave, 0)

    def merge_low(k):
        for zz in range(2):
            for bb in range(batch_count):
                at = zz * batch_count + bb
                arrived(cross.at[k, at], cross_recv.at[k, at])
                xs[k, 4 + at] = (
                    xs[k, 4 + at].astype(jnp.float32) + cross[k, at].astype(jnp.float32)
                ).astype(jnp.bfloat16)
            arrived(scross.at[k, zz], scross_recv.at[k, zz])
            hs[k, 2 + zz] = (
                hs[k, 2 + zz].astype(jnp.float32) + scross[k, zz].astype(jnp.float32)
            ).astype(jnp.bfloat16)
        give_low_corr(k, move)

    lag = 4

    @pl.when(z == 1)
    def _():
        def step(k, carry):
            @pl.when(k < steps)
            def _():
                for s in range(4):
                    arrived(xs.at[k, s], x_recv.at[k, s])
                for s in range(2):
                    arrived(hs.at[k, s], h_recv.at[k, s])
                forward_low(k, move)
                for s in range(4):
                    arrived(ws.at[k, s], w_recv.at[k, s])
                transform(k, True)
                give_low_conv(k, move)

            @pl.when(k >= lag)
            def _():
                merge_low(k - lag)

            return carry

        lax.fori_loop(0, steps + lag, step, 0)

    @pl.when(z >= 2)
    def _():
        def step(k, carry):
            @pl.when(upper_owner(k) == z)
            def _():
                for s in range(8):
                    arrived(xs.at[k, s], x_recv.at[k, s])
                for s in range(4):
                    arrived(hs.at[k, s], h_recv.at[k, s])
                    arrived(ws.at[k, s], w_recv.at[k, s])
                transform(k, False)
                give_upper(k, move)

            return carry

        lax.fori_loop(0, steps, step, 0)

    def finish_block(blk, carry):
        k = blk // batch_count
        pb = lax.rem(blk, batch_count)
        arrived(ys.at[blk], y_recv.at[blk])
        arrived(cs.at[blk], c_recv.at[blk])
        query = acts[0, blk].astype(jnp.float32)
        key = acts[1, blk].astype(jnp.float32)
        value = acts[2, blk].astype(jnp.float32)
        cot = acts[3, blk].astype(jnp.float32)
        skip = skip_ref[pl.ds(blk, 1), :]
        signal = ys[blk].astype(jnp.float32) + skip * stage[blk, 0].astype(jnp.float32)
        back = cs[blk].astype(jnp.float32) + skip * stage[blk, 1].astype(jnp.float32)
        acts[0, blk] = (query * signal).astype(jnp.bfloat16)
        acts[1, blk] = (cot * signal).astype(jnp.bfloat16)
        acts[2, blk] = (back * value).astype(jnp.bfloat16)
        acts[3, blk] = (back * key).astype(jnp.bfloat16)
        copies = output_copies(blk)
        for copy in copies[:4]:
            copy.start()
        arrived(ss.at[blk], s_recv.at[blk])

        @pl.when(pb == b)
        def _():
            remote(ss.at[blk], ss.at[blk], n_send.at[k], s_recv.at[blk], z, 1 - b).start()

        taps[blk] = factor * ss[blk].astype(jnp.float32)
        copies[4].start()
        return carry

    lax.fori_loop(0, block_count, finish_block, 0)

    def wait_gain(i, carry):
        _, _, idx = partner(i)
        arrived(gain.at[idx], g_recv.at[idx])
        arrived(gain.at[me], g_send.at[idx])
        return carry

    lax.fori_loop(0, groups - 1, wait_gain, 0)
    total = gain[0]
    for s in range(1, groups):
        total = total + gain[s]
    gs_ref[...] = factor * total

    def drain(blk, carry):
        for copy in output_copies(blk):
            copy.wait()
        give_inputs(blk, settle)
        k = blk // batch_count

        @pl.when(lax.rem(blk, batch_count) == b)
        def _():
            arrived(ss.at[blk], n_send.at[k])

            @pl.when(z == 1)
            def _():
                forward_low(k, settle)
                give_low_conv(k, settle)
                give_low_corr(k, settle)

            @pl.when(upper_owner(k) == z)
            def _():
                give_upper(k, settle)

        return carry

    lax.fori_loop(0, block_count, drain, 0)


def fused(query_proj, key_proj, value_proj, cotangent, long_filter, skip_gain):
    rows, width = query_proj.shape[1:]
    seq_count = lax.axis_size("seq")
    batch_count = lax.axis_size("dp")
    groups = seq_count * batch_count
    seq_length = seq_count * rows
    block_count = width // LANES
    steps = block_count // batch_count
    factor = (batch_count * seq_length) ** (-0.5)
    tables = transform_tables(seq_length)
    low_tables = transform_tables(seq_length // 2)
    tables = tables + (low_tables[0], low_tables[3])
    kept = tables[1].shape[0]
    signals = 2 * batch_count + 1
    half = jnp.bfloat16
    dma = pltpu.SemaphoreType.DMA
    hbm = pl.BlockSpec(memory_space=pl.ANY)
    vmem = pl.BlockSpec(memory_space=pltpu.VMEM)
    flops = 2 * steps * signals * LANES * (2 * tables[0].size * INNER // ROWS + 2 * tables[1].size)
    results = pl.pallas_call(
        functools.partial(fused_kernel, factor),
        out_shape=[jax.ShapeDtypeStruct((1, rows, width), half)] * 4
        + [
            jax.ShapeDtypeStruct((rows, width), jnp.float32),
            jax.ShapeDtypeStruct((block_count, LANES), jnp.float32),
        ],
        in_specs=[hbm] * 5 + [vmem] * 7,
        out_specs=[hbm] * 5 + [vmem],
        scratch_shapes=[
            pltpu.VMEM((4, block_count, rows, LANES), half),
            pltpu.VMEM((block_count, rows, LANES), jnp.float32),
            pltpu.VMEM((block_count, 2, rows, LANES), half),
            pltpu.VMEM((steps, rows, LANES), half),
            pltpu.VMEM((steps, groups, rows, LANES), half),
            pltpu.VMEM((steps, groups // 2, rows, LANES), half),
            pltpu.VMEM((steps, seq_count, rows, LANES), half),
            pltpu.VMEM((steps, groups // 2, rows, LANES), half),
            pltpu.VMEM((steps, seq_count // 2, rows, LANES), half),
            pltpu.VMEM((kept, 2 * INNER, signals * LANES), half),
            pltpu.VMEM((block_count, rows, LANES), half),
            pltpu.VMEM((block_count, rows, LANES), half),
            pltpu.VMEM((block_count, rows, LANES), half),
            pltpu.VMEM((groups, block_count, LANES), jnp.float32),
            dma((5, block_count)),
            dma((5, block_count)),
            dma((block_count,)),
            dma((block_count,)),
            dma((block_count,)),
            dma((steps,)),
            dma((steps,)),
            dma((steps, 3)),
            dma((steps, groups // 2)),
            dma((steps, groups)),
            dma((steps, seq_count)),
            dma((steps,)),
            dma((groups,)),
            dma((steps, groups)),
            dma((steps, groups // 2)),
            dma((steps, seq_count)),
            dma((steps, groups // 2)),
            dma((steps, seq_count // 2)),
            dma((block_count,)),
            dma((block_count,)),
            dma((block_count,)),
            dma((groups,)),
        ],
        compiler_params=pltpu.CompilerParams(
            collective_id=0, has_side_effects=True, vmem_limit_bytes=62 * 1024 * 1024
        ),
        cost_estimate=pl.CostEstimate(
            flops=flops, bytes_accessed=24 * rows * width, transcendentals=0
        ),
    )(
        query_proj, key_proj, value_proj, cotangent, long_filter,
        skip_gain.reshape(block_count, LANES), *(jnp.asarray(t) for t in tables),
    )
    return tuple(results[:5]) + (results[5].reshape(width),)


def dft_tables(seq_length):
    full_size = 2 * seq_length
    inner_size = 128
    outer_size = full_size // inner_size
    half_size = outer_size // 2
    outer_index = jnp.arange(outer_size, dtype=jnp.int32)
    half_index = jnp.arange(half_size, dtype=jnp.int32)
    inner_index = jnp.arange(inner_size, dtype=jnp.int32)
    first_angle = (
        2.0
        * math.pi
        / outer_size
        * (outer_index[:, None] * half_index[None, :] % outer_size).astype(jnp.float32)
    )
    twist_angle = (
        2.0
        * math.pi
        / full_size
        * (outer_index[:, None] * inner_index[None, :] % full_size).astype(jnp.float32)
    )
    last_angle = (
        2.0
        * math.pi
        / inner_size
        * (inner_index[:, None] * inner_index[None, :] % inner_size).astype(jnp.float32)
    )
    return (
        jnp.cos(first_angle),
        jnp.sin(first_angle),
        jnp.cos(twist_angle),
        jnp.sin(twist_angle),
        jnp.cos(last_angle),
        jnp.sin(last_angle),
    )


def forward(signal, tables):
    cos_first, sin_first, cos_twist, sin_twist, cos_last, sin_last = tables
    half_size = cos_first.shape[1]
    signal_grid = signal.reshape(signal.shape[0], half_size, 128)
    real_first = jnp.einsum("kn,rnm->rkm", cos_first, signal_grid, precision=full_precision)
    imag_first = -jnp.einsum("kn,rnm->rkm", sin_first, signal_grid, precision=full_precision)
    real_twist = real_first * cos_twist + imag_first * sin_twist
    imag_twist = imag_first * cos_twist - real_first * sin_twist
    real_last = jnp.einsum(
        "rkm,mj->rkj", real_twist, cos_last, precision=full_precision
    ) + jnp.einsum("rkm,mj->rkj", imag_twist, sin_last, precision=full_precision)
    imag_last = jnp.einsum(
        "rkm,mj->rkj", imag_twist, cos_last, precision=full_precision
    ) - jnp.einsum("rkm,mj->rkj", real_twist, sin_last, precision=full_precision)
    return (real_last, imag_last)


def inverse(real_part, imag_part, tables):
    cos_first, sin_first, cos_twist, sin_twist, cos_last, sin_last = tables
    half_size = cos_first.shape[1]
    row_total = real_part.shape[0]
    real_inner = jnp.einsum(
        "rkj,jm->rkm", real_part, cos_last, precision=full_precision
    ) - jnp.einsum("rkj,jm->rkm", imag_part, sin_last, precision=full_precision)
    imag_inner = jnp.einsum(
        "rkj,jm->rkm", imag_part, cos_last, precision=full_precision
    ) + jnp.einsum("rkj,jm->rkm", real_part, sin_last, precision=full_precision)
    real_twist = real_inner * cos_twist - imag_inner * sin_twist
    imag_twist = imag_inner * cos_twist + real_inner * sin_twist
    result = jnp.einsum(
        "kn,rkm->rnm", cos_first, real_twist, precision=full_precision
    ) - jnp.einsum("kn,rkm->rnm", sin_first, imag_twist, precision=full_precision)
    return (result / (2.0 * half_size * 128)).reshape(row_total, half_size * 128)


def filter_block(items, tables):
    mixed_blk, weighted_blk, kernel = items
    batches, chan_width, seq_length = mixed_blk.shape
    row_count = batches * chan_width
    mixed_wide = mixed_blk.astype(jnp.float32)
    weighted_wide = weighted_blk.astype(jnp.float32)
    stacked = jnp.concatenate(
        [
            mixed_wide.reshape(row_count, seq_length),
            weighted_wide.reshape(row_count, seq_length),
            kernel,
        ],
        axis=0,
    )
    real_spec, imag_spec = forward(stacked, tables)
    grid_shape = real_spec.shape[1:]
    mixed_real = real_spec[:row_count].reshape((batches, chan_width) + grid_shape)
    mixed_imag = imag_spec[:row_count].reshape((batches, chan_width) + grid_shape)
    weighted_real = real_spec[row_count : 2 * row_count].reshape((batches, chan_width) + grid_shape)
    weighted_imag = imag_spec[row_count : 2 * row_count].reshape((batches, chan_width) + grid_shape)
    kernel_real = real_spec[2 * row_count :][None]
    kernel_imag = imag_spec[2 * row_count :][None]
    conv_real = mixed_real * kernel_real - mixed_imag * kernel_imag
    conv_imag = mixed_real * kernel_imag + mixed_imag * kernel_real
    corr_real = kernel_real * weighted_real + kernel_imag * weighted_imag
    corr_imag = kernel_real * weighted_imag - kernel_imag * weighted_real
    slope_real = jnp.sum(mixed_real * weighted_real + mixed_imag * weighted_imag, axis=0)
    slope_imag = jnp.sum(mixed_real * weighted_imag - mixed_imag * weighted_real, axis=0)
    spec_real = jnp.concatenate(
        [
            conv_real.reshape((row_count,) + grid_shape),
            corr_real.reshape((row_count,) + grid_shape),
            slope_real,
        ],
        axis=0,
    )
    spec_imag = jnp.concatenate(
        [
            conv_imag.reshape((row_count,) + grid_shape),
            corr_imag.reshape((row_count,) + grid_shape),
            slope_imag,
        ],
        axis=0,
    )
    result = inverse(spec_real, spec_imag, tables)
    conv_vals = result[:row_count].reshape(batches, chan_width, seq_length).astype(jnp.bfloat16)
    corr_vals = (
        result[row_count : 2 * row_count]
        .reshape(batches, chan_width, seq_length)
        .astype(jnp.bfloat16)
    )
    slope = result[2 * row_count :]
    return (conv_vals, corr_vals, slope)


def run_blocks(mixed_rows, weighted_rows, filter_part):
    batches, part_width, seq_length = mixed_rows.shape
    block_width = min(part_width, 8)
    block_count = part_width // block_width
    tables = dft_tables(seq_length)

    def stack_rows(arr):
        return jnp.moveaxis(arr.reshape(batches, block_count, block_width, seq_length), 1, 0)

    def unstack_rows(arr):
        return jnp.moveaxis(arr, 0, 1).reshape(batches, part_width, seq_length)

    def one_block(items):
        return filter_block(items, tables)

    items = (
        stack_rows(mixed_rows),
        stack_rows(weighted_rows),
        filter_part.reshape(block_count, block_width, seq_length),
    )
    conv_vals, corr_vals, slope = lax.map(one_block, items)
    return (unstack_rows(conv_vals), unstack_rows(corr_vals), slope.reshape(part_width, seq_length))


def on_device(query_proj, key_proj, value_proj, cotangent, long_filter, skip_gain):
    rows, width = query_proj.shape[1:]
    grouped = lax.axis_size("seq") == 4 and lax.axis_size("dp") == 2
    if grouped and rows % INNER == 0 and width % (2 * LANES) == 0 and rows * width <= 2**20:
        return fused(query_proj, key_proj, value_proj, cotangent, long_filter, skip_gain)
    return spread(query_proj, key_proj, value_proj, cotangent, long_filter, skip_gain)


def spread(query_proj, key_proj, value_proj, cotangent, long_filter, skip_gain):
    query_rows = query_proj[0].astype(jnp.float32)
    key_rows = key_proj[0].astype(jnp.float32)
    value_rows = value_proj[0].astype(jnp.float32)
    cot_rows = cotangent[0].astype(jnp.float32)
    local_length = query_proj.shape[1]
    chan_width = query_proj.shape[2]
    seq_count = lax.axis_size("seq")
    batch_count = lax.axis_size("dp")
    factor = (batch_count * seq_count * local_length) ** (-0.5)
    mixed = (key_rows * value_rows).astype(jnp.bfloat16)
    weighted = (cot_rows * query_rows).astype(jnp.bfloat16)
    mixed_wide = mixed.astype(jnp.float32)
    weighted_wide = weighted.astype(jnp.float32)
    gain_term = factor * jnp.sum(weighted_wide * mixed_wide, axis=0)
    grad_skip = lax.psum(gain_term, ("seq", "dp"))
    filter_share = lax.all_to_all(long_filter.T, "seq", split_axis=0, concat_axis=1, tiled=True)
    groups = seq_count * batch_count
    share_width = chan_width // groups
    mixed_cols, weighted_cols = (
        lax.all_to_all(mixed.T, ("seq", "dp"), split_axis=0, concat_axis=1, tiled=True),
        lax.all_to_all(weighted.T, ("seq", "dp"), split_axis=0, concat_axis=1, tiled=True),
    )

    def to_sequences(arr):
        arr = arr.reshape(share_width, seq_count, batch_count, local_length)
        return jnp.transpose(arr, (2, 0, 1, 3)).reshape(
            batch_count, share_width, seq_count * local_length
        )

    def to_pieces(arr):
        arr = arr.reshape(batch_count, share_width, seq_count, local_length)
        return jnp.transpose(arr, (1, 2, 0, 3)).reshape(share_width, groups * local_length)

    filter_part = lax.dynamic_slice_in_dim(
        filter_share, lax.axis_index("dp") * share_width, share_width, 0
    )
    conv_vals, corr_vals, slope = run_blocks(
        to_sequences(mixed_cols), to_sequences(weighted_cols), filter_part
    )
    conv_back, corr_back = (
        lax.all_to_all(
            to_pieces(conv_vals), ("seq", "dp"), split_axis=1, concat_axis=0, tiled=True
        ),
        lax.all_to_all(
            to_pieces(corr_vals), ("seq", "dp"), split_axis=1, concat_axis=0, tiled=True
        ),
    )
    slope_share = lax.all_gather(slope, "dp", axis=0, tiled=True)
    slope_rows = lax.all_to_all(slope_share, "seq", split_axis=1, concat_axis=0, tiled=True)
    grad_filter = factor * slope_rows.T
    conv_rows = conv_back.T.astype(jnp.float32)
    corr_rows = corr_back.T.astype(jnp.float32)
    signal = conv_rows + skip_gain[None, :] * mixed_wide
    output = (query_rows * signal).astype(jnp.bfloat16)
    grad_query = (cot_rows * signal).astype(jnp.bfloat16)
    back = corr_rows + skip_gain[None, :] * weighted_wide
    grad_key = (back * value_rows).astype(jnp.bfloat16)
    grad_value = (back * key_rows).astype(jnp.bfloat16)
    return (
        output[None],
        grad_query[None],
        grad_key[None],
        grad_value[None],
        grad_filter,
        grad_skip,
    )


def solution(mesh):
    return jax.shard_map(
        on_device,
        mesh=mesh,
        in_specs=(
            P("dp", "seq", "chan"),
            P("dp", "seq", "chan"),
            P("dp", "seq", "chan"),
            P("dp", "seq", "chan"),
            P("seq", "chan"),
            P("chan"),
        ),
        out_specs=(
            P("dp", "seq", "chan"),
            P("dp", "seq", "chan"),
            P("dp", "seq", "chan"),
            P("dp", "seq", "chan"),
            P("seq", "chan"),
            P("chan"),
        ),
        check_vma=False,
    )
```

```python
import functools
import math

import jax
import jax.numpy as jnp
import ml_dtypes
import numpy as np
from jax import lax
from jax.experimental import pallas as pl
from jax.experimental.pallas import tpu as pltpu
from jax.sharding import PartitionSpec as P

full_precision = lax.Precision.HIGHEST
MESH = pl.DeviceIdType.MESH
LANES = 128
INNER = 128
ROWS = 16


def transform_tables(seq_length):
    full_size = 2 * seq_length
    outer = full_size // INNER
    firsts = outer // 2
    kept = outer // 2 + 1
    k1 = np.arange(kept)
    n1 = np.arange(firsts)
    first = 2.0 * np.pi * (k1[:, None] * n1[None, :] % outer) / outer
    first_parts = np.stack([np.cos(first), -np.sin(first)], axis=1).reshape(2 * kept, firsts)
    live = np.ones(2 * kept, bool)
    live[[1, 2 * kept - 1]] = False
    enter = np.kron(first_parts[live], np.eye(ROWS))
    weight = np.where((k1 == 0) | (k1 == outer // 2), 1.0, 2.0) / full_size
    leave = np.kron((first_parts.reshape(kept, 2, firsts) * weight[:, None, None]).reshape(2 * kept, firsts)[live].T, np.eye(ROWS))
    n2 = np.arange(INNER)
    k2 = np.arange(INNER)
    freq = k1[:, None, None] + outer * k2[None, :, None]
    angle = 2.0 * np.pi * (freq * n2[None, None, :] % full_size) / full_size
    cos, sin = np.cos(angle), np.sin(angle)
    middle = np.concatenate(
        [np.concatenate([cos, sin], axis=2), np.concatenate([-sin, cos], axis=2)], axis=1
    )
    back = np.transpose(middle, (0, 2, 1))
    return tuple(np.asarray(t).astype(ml_dtypes.bfloat16) for t in (enter, middle, back, leave))


def fused_kernel(
    factor,
    q_hbm, k_hbm, v_hbm, ct_hbm, taps_hbm, skip_ref, enter_ref, middle_ref, back_ref, leave_ref, enter_low_ref, leave_low_ref,
    out_hbm, gq_hbm, gk_hbm, gv_hbm, gf_hbm, gs_ref,
    acts, taps, stage, hstage, xs, ws, hs, cross, scross, spec, ys, cs, ss, gain,
    in_sem, out_sem, x_send, x2_send, w_send, h_send, h2_send, f_send, y_send, c_send, s_send, n_send, g_send,
    x_recv, w_recv, h_recv, cross_recv, scross_recv, y_recv, c_recv, s_recv, g_recv,
):
    z = lax.axis_index("seq")
    b = lax.axis_index("dp")
    seq_count, batch_count = 4, 2
    groups = seq_count * batch_count
    me = z * batch_count + b
    block_count, rows = acts.shape[1], acts.shape[2]
    steps = block_count // batch_count
    per_row = rows // INNER
    act_in = (q_hbm, k_hbm, v_hbm, ct_hbm)
    act_out = (out_hbm, gq_hbm, gk_hbm, gv_hbm)

    def partner(i):
        pz = lax.rem(z + 1 + i // batch_count, seq_count)
        pb = lax.rem(b + 1 + lax.rem(i, batch_count), batch_count)
        return pz, pb, pz * batch_count + pb

    def cols(blk):
        return pl.ds(pl.multiple_of(blk * LANES, LANES), LANES)

    def upper_owner(k):
        return jnp.where(jnp.logical_or(k == 1, k == 3), 3, 2)

    def merge_order(m):
        order = [0, 2, 4, 5, 1, 3] + list(range(6, steps))
        k = 0
        for i, step in enumerate(order):
            k = k + jnp.where(m == i, step, 0)
        return k

    def input_copies(blk):
        found = [
            pltpu.make_async_copy(act_in[a].at[0, :, cols(blk)], acts.at[a, blk], in_sem.at[a, blk])
            for a in range(4)
        ]
        found.append(pltpu.make_async_copy(taps_hbm.at[:, cols(blk)], taps.at[blk], in_sem.at[4, blk]))
        return found

    def output_copies(blk):
        found = [
            pltpu.make_async_copy(acts.at[a, blk], act_out[a].at[0, :, cols(blk)], out_sem.at[a, blk])
            for a in range(4)
        ]
        found.append(pltpu.make_async_copy(taps.at[blk], gf_hbm.at[:, cols(blk)], out_sem.at[4, blk]))
        return found

    def start_input(blk, carry):
        for copy in input_copies(blk):
            copy.start()
        return carry

    lax.fori_loop(0, block_count, start_input, 0)

    barrier = pltpu.get_barrier_semaphore()

    def greet(i, carry):
        pz, pb, _ = partner(i)
        pl.semaphore_signal(barrier, inc=1, device_id={"seq": pz, "dp": pb}, device_id_type=MESH)
        return carry

    lax.fori_loop(0, groups - 1, greet, 0)
    pl.semaphore_wait(barrier, groups - 1)

    def remote(src, dst, send, recv, pz, pb):
        return pltpu.make_async_remote_copy(
            src_ref=src, dst_ref=dst, send_sem=send, recv_sem=recv,
            device_id={"seq": pz, "dp": pb}, device_id_type=MESH,
        )

    def arrived(ref, sem):
        pltpu.make_async_copy(ref, ref, sem).wait()

    def move(src, dst, send, recv, pz, pb):
        here = jnp.logical_and(pz == z, pb == b)

        @pl.when(here)
        def _():
            pltpu.make_async_copy(src, dst, recv).start()

        @pl.when(jnp.logical_not(here))
        def _():
            remote(src, dst, send, recv, pz, pb).start()

    def settle(src, dst, send, recv, pz, pb):
        @pl.when(jnp.logical_not(jnp.logical_and(pz == z, pb == b)))
        def _():
            arrived(src, send)

    def give_inputs(blk, act):
        k = blk // batch_count
        pb = lax.rem(blk, batch_count)
        owner = upper_owner(k)
        target = jnp.where(z < 2, 1, owner)
        slot = lax.rem(z, 2) * batch_count + b
        act(stage.at[blk, 0], xs.at[k, me], x_send.at[blk], x_recv.at[k, me], target, pb)

        @pl.when(pb == b)
        def _():
            act(hstage.at[k], hs.at[k, z], h_send.at[k], h_recv.at[k, z], target, b)

        act(stage.at[blk, 1], ws.at[k, slot], w_send.at[blk], w_recv.at[k, slot], target, pb)

    def give_across(k, act):
        owner = upper_owner(k)
        for pb in range(batch_count):
            blk = k * batch_count + pb
            act(stage.at[blk, 0], xs.at[k, me], x2_send.at[blk], x_recv.at[k, me], owner, pb)
        act(hstage.at[k], hs.at[k, z], h2_send.at[k], h_recv.at[k, z], owner, b)

    def forward_low(k, act):
        owner = upper_owner(k)
        for bb in range(batch_count):
            act(xs.at[k, bb], xs.at[k, bb], f_send.at[k, bb], x_recv.at[k, bb], owner, b)
        act(hs.at[k, 0], hs.at[k, 0], f_send.at[k, 2], h_recv.at[k, 0], owner, b)

    def give_upper(k, act):
        blk = k * batch_count + b
        for zz in range(2):
            for bb in range(batch_count):
                at = zz * batch_count + bb
                act(xs.at[k, at], cross.at[k, at], c_send.at[k, at], cross_recv.at[k, at], 1, b)
            act(hs.at[k, zz], scross.at[k, zz], s_send.at[k, zz], scross_recv.at[k, zz], 1, b)
        for zz in range(2, 4):
            for bb in range(batch_count):
                at = zz * batch_count + bb
                low = at - 2 * batch_count
                act(ws.at[k, low], ys.at[blk], y_send.at[k, low], y_recv.at[blk], zz, bb)
                act(xs.at[k, at], cs.at[blk], c_send.at[k, at], c_recv.at[blk], zz, bb)
            act(hs.at[k, zz], ss.at[blk], s_send.at[k, zz], s_recv.at[blk], zz, b)

    def give_low_conv(k, act):
        blk = k * batch_count + b
        for zz in range(2):
            for bb in range(batch_count):
                at = zz * batch_count + bb
                act(ws.at[k, at], ys.at[blk], y_send.at[k, at], y_recv.at[blk], zz, bb)

    def give_low_corr(k, act):
        blk = k * batch_count + b
        for zz in range(2):
            for bb in range(batch_count):
                at = zz * batch_count + bb
                act(xs.at[k, 4 + at], cs.at[blk], c_send.at[k, at], c_recv.at[blk], zz, bb)
            act(hs.at[k, 2 + zz], ss.at[blk], s_send.at[k, zz], s_recv.at[blk], zz, b)

    ahead = 2

    def send_block(blk, carry):
        for copy in input_copies(blk):
            copy.wait()
        mixed = (acts[1, blk].astype(jnp.float32) * acts[2, blk].astype(jnp.float32)).astype(jnp.bfloat16)
        weighted = (acts[3, blk].astype(jnp.float32) * acts[0, blk].astype(jnp.float32)).astype(jnp.bfloat16)
        stage[blk, 0] = mixed
        stage[blk, 1] = weighted
        gain[me, pl.ds(blk, 1), :] = jnp.sum(
            weighted.astype(jnp.float32) * mixed.astype(jnp.float32), axis=0, keepdims=True
        )

        @pl.when(lax.rem(blk, batch_count) == b)
        def _():
            hstage[blk // batch_count] = taps[blk].astype(jnp.bfloat16)

        give_inputs(blk, move)

        @pl.when(jnp.logical_and(z == 1, jnp.logical_and(lax.rem(blk, 2) == 1, blk < 2 * ahead)))
        def _():
            give_across(blk // batch_count, move)

        return carry

    lax.fori_loop(0, block_count, send_block, 0)

    def send_gain(i, carry):
        pz, pb, idx = partner(i)
        remote(gain.at[me], gain.at[me], g_send.at[idx], g_recv.at[me], pz, pb).start()
        return carry

    lax.fori_loop(0, groups - 1, send_gain, 0)

    def transform(k, low):
        kept = (middle_ref.shape[0] + 1) // 2 if low else middle_ref.shape[0]
        firsts = (2 if low else 4) * per_row
        enter_table = enter_low_ref if low else enter_ref
        leave_table = leave_low_ref if low else leave_ref
        scale = 2 if low else 1
        live = [(k1, part) for k1 in range(kept) for part in range(2) if part == 0 or 0 < k1 < kept - 1]
        for k1 in (0, kept - 1):
            spec[k1, INNER:, :] = jnp.zeros((INNER, spec.shape[2]), jnp.bfloat16)

        def enter(g, inner):
            def piece(ref):
                return jnp.concatenate(
                    [
                        ref(n1 // per_row, pl.ds(pl.multiple_of(n1 % per_row * INNER + g * ROWS, ROWS), ROWS))
                        for n1 in range(firsts)
                    ],
                    axis=0,
                )

            def weighted_rows(s, r, bb):
                if low:
                    return ws[k, s * batch_count + bb, r, :]
                if s < 2:
                    return jnp.zeros((ROWS, LANES), jnp.bfloat16)
                return ws[k, (s - 2) * batch_count + bb, r, :]

            signals = [
                piece(lambda s, r, bb=bb: xs[k, s * batch_count + bb, r, :]) for bb in range(batch_count)
            ]
            signals += [piece(lambda s, r, bb=bb: weighted_rows(s, r, bb)) for bb in range(batch_count)]
            signals.append(piece(lambda s, r: hs[k, s, r, :]))
            stacked = jnp.concatenate(signals, axis=1)
            grid = jnp.dot(enter_table[...], stacked, preferred_element_type=jnp.float32).astype(jnp.bfloat16)
            for i, (k1, part) in enumerate(live):
                at = i * ROWS
                spec[k1, pl.ds(pl.multiple_of(part * INNER + g * ROWS, ROWS), ROWS), :] = grid[at : at + ROWS]
            return inner

        lax.fori_loop(0, INNER // ROWS, enter, 0)

        def products(full):
            real, imag = full[:INNER], full[INNER:]

            def take(i):
                return real[:, i * LANES : (i + 1) * LANES], imag[:, i * LANES : (i + 1) * LANES]

            hr, hi = take(2 * batch_count)
            out_real, out_imag = [], []
            for bb in range(batch_count):
                mr, mi = take(bb)
                out_real.append(mr * hr - mi * hi)
                out_imag.append(mr * hi + mi * hr)
            for bb in range(batch_count):
                wr, wi = take(batch_count + bb)
                out_real.append(hr * wr + hi * wi)
                out_imag.append(hr * wi - hi * wr)
            slope_real, slope_imag = 0.0, 0.0
            for bb in range(batch_count):
                mr, mi = take(bb)
                wr, wi = take(batch_count + bb)
                slope_real = slope_real + (mr * wr + mi * wi)
                slope_imag = slope_imag + (mr * wi - mi * wr)
            out_real.append(slope_real)
            out_imag.append(slope_imag)
            return jnp.concatenate(
                [
                    jnp.concatenate([t.astype(jnp.bfloat16) for t in out_real], axis=1),
                    jnp.concatenate([t.astype(jnp.bfloat16) for t in out_imag], axis=1),
                ],
                axis=0,
            )

        def middle(firsts_now):
            fulls = [
                jnp.dot(middle_ref[scale * k1], spec[k1], preferred_element_type=jnp.float32) for k1 in firsts_now
            ]
            turned = [products(full) for full in fulls]
            backs = [
                jnp.dot(back_ref[scale * k1], turn, preferred_element_type=jnp.float32).astype(jnp.bfloat16)
                for k1, turn in zip(firsts_now, turned)
            ]
            for k1, back in zip(firsts_now, backs):
                spec[k1] = back

        def middle_pair(p, inner):
            middle([2 * p, 2 * p + 1])
            return inner

        lax.fori_loop(0, kept // 2, middle_pair, 0)
        middle([kept - 1])

        def leave(g, inner):
            stacked = jnp.concatenate(
                [
                    spec[k1, pl.ds(pl.multiple_of(part * INNER + g * ROWS, ROWS), ROWS), :]
                    for k1, part in live
                ],
                axis=0,
            )
            grid = jnp.dot(leave_table[...], stacked, preferred_element_type=jnp.float32).astype(jnp.bfloat16)
            for n1 in range(firsts):
                s = n1 // per_row
                r = pl.ds(pl.multiple_of(n1 % per_row * INNER + g * ROWS, ROWS), ROWS)
                part = grid[n1 * ROWS : (n1 + 1) * ROWS]
                for bb in range(batch_count):
                    if low:
                        ws[k, s * batch_count + bb, r, :] = part[:, bb * LANES : (bb + 1) * LANES]
                    elif s >= 2:
                        ws[k, (s - 2) * batch_count + bb, r, :] = part[:, bb * LANES : (bb + 1) * LANES]
                    at = batch_count + bb
                    to = s * batch_count + bb + (4 if low else 0)
                    xs[k, to, r, :] = part[:, at * LANES : (at + 1) * LANES]
                hs[k, s + (2 if low else 0), r, :] = part[:, 2 * batch_count * LANES :]
            return inner

        lax.fori_loop(0, INNER // ROWS, leave, 0)

    def merge_low(k):
        for zz in range(2):
            for bb in range(batch_count):
                at = zz * batch_count + bb
                arrived(cross.at[k, at], cross_recv.at[k, at])
                xs[k, 4 + at] = (
                    xs[k, 4 + at].astype(jnp.float32) + cross[k, at].astype(jnp.float32)
                ).astype(jnp.bfloat16)
            arrived(scross.at[k, zz], scross_recv.at[k, zz])
            hs[k, 2 + zz] = (
                hs[k, 2 + zz].astype(jnp.float32) + scross[k, zz].astype(jnp.float32)
            ).astype(jnp.bfloat16)
        give_low_corr(k, move)

    def finish_block(blk, carry):
        k = blk // batch_count
        pb = lax.rem(blk, batch_count)
        arrived(ys.at[blk], y_recv.at[blk])
        arrived(cs.at[blk], c_recv.at[blk])
        query = acts[0, blk].astype(jnp.float32)
        key = acts[1, blk].astype(jnp.float32)
        value = acts[2, blk].astype(jnp.float32)
        cot = acts[3, blk].astype(jnp.float32)
        skip = skip_ref[pl.ds(blk, 1), :]
        signal = ys[blk].astype(jnp.float32) + skip * stage[blk, 0].astype(jnp.float32)
        back = cs[blk].astype(jnp.float32) + skip * stage[blk, 1].astype(jnp.float32)
        acts[0, blk] = (query * signal).astype(jnp.bfloat16)
        acts[1, blk] = (cot * signal).astype(jnp.bfloat16)
        acts[2, blk] = (back * value).astype(jnp.bfloat16)
        acts[3, blk] = (back * key).astype(jnp.bfloat16)
        copies = output_copies(blk)
        for copy in copies[:4]:
            copy.start()
        arrived(ss.at[blk], s_recv.at[blk])

        @pl.when(pb == b)
        def _():
            remote(ss.at[blk], ss.at[blk], n_send.at[k], s_recv.at[blk], z, 1 - b).start()

        taps[blk] = factor * ss[blk].astype(jnp.float32)
        copies[4].start()
        return carry

    def finish_step(k):
        for bb in range(batch_count):
            finish_block(k * batch_count + lax.rem(b + bb, batch_count), 0)

    def finish_rest(m, carry):
        finish_step(merge_order(m))
        return carry

    lag = 5
    wait_upper = 4

    @pl.when(z == 0)
    def _():
        lax.fori_loop(0, steps, finish_rest, 0)

    @pl.when(z == 1)
    def _():
        def step(k, carry):
            @pl.when(k < steps)
            def _():
                for s in range(4):
                    arrived(xs.at[k, s], x_recv.at[k, s])
                for s in range(2):
                    arrived(hs.at[k, s], h_recv.at[k, s])
                forward_low(k, move)

                @pl.when(k < steps - ahead)
                def _():
                    give_across(k + ahead, move)

                for s in range(4):
                    arrived(ws.at[k, s], w_recv.at[k, s])
                transform(k, True)
                give_low_conv(k, move)

            @pl.when(k >= lag)
            def _():
                merge_low(merge_order(k - lag))

            @pl.when(k >= lag + 1)
            def _():
                finish_step(merge_order(k - lag - 1))

            return carry

        lax.fori_loop(0, steps + lag, step, 0)
        finish_step(merge_order(steps - 1))

    @pl.when(z >= 2)
    def _():
        def step(k, carry):
            @pl.when(upper_owner(k) == z)
            def _():
                for s in range(8):
                    arrived(xs.at[k, s], x_recv.at[k, s])
                for s in range(4):
                    arrived(hs.at[k, s], h_recv.at[k, s])
                    arrived(ws.at[k, s], w_recv.at[k, s])
                transform(k, False)
                give_upper(k, move)

            @pl.when(k >= wait_upper)
            def _():
                finish_step(merge_order(k - wait_upper))

            return carry

        lax.fori_loop(0, steps, step, 0)

        def rest(m, carry):
            finish_step(merge_order(m))
            return carry

        lax.fori_loop(steps - wait_upper, steps, rest, 0)

    def wait_gain(i, carry):
        _, _, idx = partner(i)
        arrived(gain.at[idx], g_recv.at[idx])
        arrived(gain.at[me], g_send.at[idx])
        return carry

    lax.fori_loop(0, groups - 1, wait_gain, 0)
    total = gain[0]
    for s in range(1, groups):
        total = total + gain[s]
    gs_ref[...] = factor * total

    def drain(blk, carry):
        for copy in output_copies(blk):
            copy.wait()
        give_inputs(blk, settle)
        k = blk // batch_count

        @pl.when(lax.rem(blk, batch_count) == b)
        def _():
            arrived(ss.at[blk], n_send.at[k])

            @pl.when(z == 1)
            def _():
                give_across(k, settle)
                forward_low(k, settle)
                give_low_conv(k, settle)
                give_low_corr(k, settle)

            @pl.when(upper_owner(k) == z)
            def _():
                give_upper(k, settle)

        return carry

    lax.fori_loop(0, block_count, drain, 0)


def fused(query_proj, key_proj, value_proj, cotangent, long_filter, skip_gain):
    rows, width = query_proj.shape[1:]
    seq_count = lax.axis_size("seq")
    batch_count = lax.axis_size("dp")
    groups = seq_count * batch_count
    seq_length = seq_count * rows
    block_count = width // LANES
    steps = block_count // batch_count
    factor = (batch_count * seq_length) ** (-0.5)
    tables = transform_tables(seq_length)
    low_tables = transform_tables(seq_length // 2)
    tables = tables + (low_tables[0], low_tables[3])
    kept = tables[1].shape[0]
    signals = 2 * batch_count + 1
    half = jnp.bfloat16
    dma = pltpu.SemaphoreType.DMA
    hbm = pl.BlockSpec(memory_space=pl.ANY)
    vmem = pl.BlockSpec(memory_space=pltpu.VMEM)
    flops = 2 * steps * signals * LANES * (2 * tables[0].size * INNER // ROWS + 2 * tables[1].size)
    results = pl.pallas_call(
        functools.partial(fused_kernel, factor),
        out_shape=[jax.ShapeDtypeStruct((1, rows, width), half)] * 4
        + [
            jax.ShapeDtypeStruct((rows, width), jnp.float32),
            jax.ShapeDtypeStruct((block_count, LANES), jnp.float32),
        ],
        in_specs=[hbm] * 5 + [vmem] * 7,
        out_specs=[hbm] * 5 + [vmem],
        scratch_shapes=[
            pltpu.VMEM((4, block_count, rows, LANES), half),
            pltpu.VMEM((block_count, rows, LANES), jnp.float32),
            pltpu.VMEM((block_count, 2, rows, LANES), half),
            pltpu.VMEM((steps, rows, LANES), half),
            pltpu.VMEM((steps, groups, rows, LANES), half),
            pltpu.VMEM((steps, groups // 2, rows, LANES), half),
            pltpu.VMEM((steps, seq_count, rows, LANES), half),
            pltpu.VMEM((steps, groups // 2, rows, LANES), half),
            pltpu.VMEM((steps, seq_count // 2, rows, LANES), half),
            pltpu.VMEM((kept, 2 * INNER, signals * LANES), half),
            pltpu.VMEM((block_count, rows, LANES), half),
            pltpu.VMEM((block_count, rows, LANES), half),
            pltpu.VMEM((block_count, rows, LANES), half),
            pltpu.VMEM((groups, block_count, LANES), jnp.float32),
            dma((5, block_count)),
            dma((5, block_count)),
            dma((block_count,)),
            dma((block_count,)),
            dma((block_count,)),
            dma((steps,)),
            dma((steps,)),
            dma((steps, 3)),
            dma((steps, groups // 2)),
            dma((steps, groups)),
            dma((steps, seq_count)),
            dma((steps,)),
            dma((groups,)),
            dma((steps, groups)),
            dma((steps, groups // 2)),
            dma((steps, seq_count)),
            dma((steps, groups // 2)),
            dma((steps, seq_count // 2)),
            dma((block_count,)),
            dma((block_count,)),
            dma((block_count,)),
            dma((groups,)),
        ],
        compiler_params=pltpu.CompilerParams(
            collective_id=0, has_side_effects=True, vmem_limit_bytes=62 * 1024 * 1024
        ),
        cost_estimate=pl.CostEstimate(
            flops=flops, bytes_accessed=24 * rows * width, transcendentals=0
        ),
    )(
        query_proj, key_proj, value_proj, cotangent, long_filter,
        skip_gain.reshape(block_count, LANES), *(jnp.asarray(t) for t in tables),
    )
    return tuple(results[:5]) + (results[5].reshape(width),)


def dft_tables(seq_length):
    full_size = 2 * seq_length
    inner_size = 128
    outer_size = full_size // inner_size
    half_size = outer_size // 2
    outer_index = jnp.arange(outer_size, dtype=jnp.int32)
    half_index = jnp.arange(half_size, dtype=jnp.int32)
    inner_index = jnp.arange(inner_size, dtype=jnp.int32)
    first_angle = (
        2.0
        * math.pi
        / outer_size
        * (outer_index[:, None] * half_index[None, :] % outer_size).astype(jnp.float32)
    )
    twist_angle = (
        2.0
        * math.pi
        / full_size
        * (outer_index[:, None] * inner_index[None, :] % full_size).astype(jnp.float32)
    )
    last_angle = (
        2.0
        * math.pi
        / inner_size
        * (inner_index[:, None] * inner_index[None, :] % inner_size).astype(jnp.float32)
    )
    return (
        jnp.cos(first_angle),
        jnp.sin(first_angle),
        jnp.cos(twist_angle),
        jnp.sin(twist_angle),
        jnp.cos(last_angle),
        jnp.sin(last_angle),
    )


def forward(signal, tables):
    cos_first, sin_first, cos_twist, sin_twist, cos_last, sin_last = tables
    half_size = cos_first.shape[1]
    signal_grid = signal.reshape(signal.shape[0], half_size, 128)
    real_first = jnp.einsum("kn,rnm->rkm", cos_first, signal_grid, precision=full_precision)
    imag_first = -jnp.einsum("kn,rnm->rkm", sin_first, signal_grid, precision=full_precision)
    real_twist = real_first * cos_twist + imag_first * sin_twist
    imag_twist = imag_first * cos_twist - real_first * sin_twist
    real_last = jnp.einsum(
        "rkm,mj->rkj", real_twist, cos_last, precision=full_precision
    ) + jnp.einsum("rkm,mj->rkj", imag_twist, sin_last, precision=full_precision)
    imag_last = jnp.einsum(
        "rkm,mj->rkj", imag_twist, cos_last, precision=full_precision
    ) - jnp.einsum("rkm,mj->rkj", real_twist, sin_last, precision=full_precision)
    return (real_last, imag_last)


def inverse(real_part, imag_part, tables):
    cos_first, sin_first, cos_twist, sin_twist, cos_last, sin_last = tables
    half_size = cos_first.shape[1]
    row_total = real_part.shape[0]
    real_inner = jnp.einsum(
        "rkj,jm->rkm", real_part, cos_last, precision=full_precision
    ) - jnp.einsum("rkj,jm->rkm", imag_part, sin_last, precision=full_precision)
    imag_inner = jnp.einsum(
        "rkj,jm->rkm", imag_part, cos_last, precision=full_precision
    ) + jnp.einsum("rkj,jm->rkm", real_part, sin_last, precision=full_precision)
    real_twist = real_inner * cos_twist - imag_inner * sin_twist
    imag_twist = imag_inner * cos_twist + real_inner * sin_twist
    result = jnp.einsum(
        "kn,rkm->rnm", cos_first, real_twist, precision=full_precision
    ) - jnp.einsum("kn,rkm->rnm", sin_first, imag_twist, precision=full_precision)
    return (result / (2.0 * half_size * 128)).reshape(row_total, half_size * 128)


def filter_block(items, tables):
    mixed_blk, weighted_blk, kernel = items
    batches, chan_width, seq_length = mixed_blk.shape
    row_count = batches * chan_width
    mixed_wide = mixed_blk.astype(jnp.float32)
    weighted_wide = weighted_blk.astype(jnp.float32)
    stacked = jnp.concatenate(
        [
            mixed_wide.reshape(row_count, seq_length),
            weighted_wide.reshape(row_count, seq_length),
            kernel,
        ],
        axis=0,
    )
    real_spec, imag_spec = forward(stacked, tables)
    grid_shape = real_spec.shape[1:]
    mixed_real = real_spec[:row_count].reshape((batches, chan_width) + grid_shape)
    mixed_imag = imag_spec[:row_count].reshape((batches, chan_width) + grid_shape)
    weighted_real = real_spec[row_count : 2 * row_count].reshape((batches, chan_width) + grid_shape)
    weighted_imag = imag_spec[row_count : 2 * row_count].reshape((batches, chan_width) + grid_shape)
    kernel_real = real_spec[2 * row_count :][None]
    kernel_imag = imag_spec[2 * row_count :][None]
    conv_real = mixed_real * kernel_real - mixed_imag * kernel_imag
    conv_imag = mixed_real * kernel_imag + mixed_imag * kernel_real
    corr_real = kernel_real * weighted_real + kernel_imag * weighted_imag
    corr_imag = kernel_real * weighted_imag - kernel_imag * weighted_real
    slope_real = jnp.sum(mixed_real * weighted_real + mixed_imag * weighted_imag, axis=0)
    slope_imag = jnp.sum(mixed_real * weighted_imag - mixed_imag * weighted_real, axis=0)
    spec_real = jnp.concatenate(
        [
            conv_real.reshape((row_count,) + grid_shape),
            corr_real.reshape((row_count,) + grid_shape),
            slope_real,
        ],
        axis=0,
    )
    spec_imag = jnp.concatenate(
        [
            conv_imag.reshape((row_count,) + grid_shape),
            corr_imag.reshape((row_count,) + grid_shape),
            slope_imag,
        ],
        axis=0,
    )
    result = inverse(spec_real, spec_imag, tables)
    conv_vals = result[:row_count].reshape(batches, chan_width, seq_length).astype(jnp.bfloat16)
    corr_vals = (
        result[row_count : 2 * row_count]
        .reshape(batches, chan_width, seq_length)
        .astype(jnp.bfloat16)
    )
    slope = result[2 * row_count :]
    return (conv_vals, corr_vals, slope)


def run_blocks(mixed_rows, weighted_rows, filter_part):
    batches, part_width, seq_length = mixed_rows.shape
    block_width = min(part_width, 8)
    block_count = part_width // block_width
    tables = dft_tables(seq_length)

    def stack_rows(arr):
        return jnp.moveaxis(arr.reshape(batches, block_count, block_width, seq_length), 1, 0)

    def unstack_rows(arr):
        return jnp.moveaxis(arr, 0, 1).reshape(batches, part_width, seq_length)

    def one_block(items):
        return filter_block(items, tables)

    items = (
        stack_rows(mixed_rows),
        stack_rows(weighted_rows),
        filter_part.reshape(block_count, block_width, seq_length),
    )
    conv_vals, corr_vals, slope = lax.map(one_block, items)
    return (unstack_rows(conv_vals), unstack_rows(corr_vals), slope.reshape(part_width, seq_length))


def on_device(query_proj, key_proj, value_proj, cotangent, long_filter, skip_gain):
    rows, width = query_proj.shape[1:]
    grouped = lax.axis_size("seq") == 4 and lax.axis_size("dp") == 2
    if grouped and rows % INNER == 0 and width >= 16 * LANES and width % (2 * LANES) == 0 and rows * width <= 2**20:
        return fused(query_proj, key_proj, value_proj, cotangent, long_filter, skip_gain)
    return spread(query_proj, key_proj, value_proj, cotangent, long_filter, skip_gain)


def spread(query_proj, key_proj, value_proj, cotangent, long_filter, skip_gain):
    query_rows = query_proj[0].astype(jnp.float32)
    key_rows = key_proj[0].astype(jnp.float32)
    value_rows = value_proj[0].astype(jnp.float32)
    cot_rows = cotangent[0].astype(jnp.float32)
    local_length = query_proj.shape[1]
    chan_width = query_proj.shape[2]
    seq_count = lax.axis_size("seq")
    batch_count = lax.axis_size("dp")
    factor = (batch_count * seq_count * local_length) ** (-0.5)
    mixed = (key_rows * value_rows).astype(jnp.bfloat16)
    weighted = (cot_rows * query_rows).astype(jnp.bfloat16)
    mixed_wide = mixed.astype(jnp.float32)
    weighted_wide = weighted.astype(jnp.float32)
    gain_term = factor * jnp.sum(weighted_wide * mixed_wide, axis=0)
    grad_skip = lax.psum(gain_term, ("seq", "dp"))
    filter_share = lax.all_to_all(long_filter.T, "seq", split_axis=0, concat_axis=1, tiled=True)
    groups = seq_count * batch_count
    share_width = chan_width // groups
    mixed_cols, weighted_cols = (
        lax.all_to_all(mixed.T, ("seq", "dp"), split_axis=0, concat_axis=1, tiled=True),
        lax.all_to_all(weighted.T, ("seq", "dp"), split_axis=0, concat_axis=1, tiled=True),
    )

    def to_sequences(arr):
        arr = arr.reshape(share_width, seq_count, batch_count, local_length)
        return jnp.transpose(arr, (2, 0, 1, 3)).reshape(
            batch_count, share_width, seq_count * local_length
        )

    def to_pieces(arr):
        arr = arr.reshape(batch_count, share_width, seq_count, local_length)
        return jnp.transpose(arr, (1, 2, 0, 3)).reshape(share_width, groups * local_length)

    filter_part = lax.dynamic_slice_in_dim(
        filter_share, lax.axis_index("dp") * share_width, share_width, 0
    )
    conv_vals, corr_vals, slope = run_blocks(
        to_sequences(mixed_cols), to_sequences(weighted_cols), filter_part
    )
    conv_back, corr_back = (
        lax.all_to_all(
            to_pieces(conv_vals), ("seq", "dp"), split_axis=1, concat_axis=0, tiled=True
        ),
        lax.all_to_all(
            to_pieces(corr_vals), ("seq", "dp"), split_axis=1, concat_axis=0, tiled=True
        ),
    )
    slope_share = lax.all_gather(slope, "dp", axis=0, tiled=True)
    slope_rows = lax.all_to_all(slope_share, "seq", split_axis=1, concat_axis=0, tiled=True)
    grad_filter = factor * slope_rows.T
    conv_rows = conv_back.T.astype(jnp.float32)
    corr_rows = corr_back.T.astype(jnp.float32)
    signal = conv_rows + skip_gain[None, :] * mixed_wide
    output = (query_rows * signal).astype(jnp.bfloat16)
    grad_query = (cot_rows * signal).astype(jnp.bfloat16)
    back = corr_rows + skip_gain[None, :] * weighted_wide
    grad_key = (back * value_rows).astype(jnp.bfloat16)
    grad_value = (back * key_rows).astype(jnp.bfloat16)
    return (
        output[None],
        grad_query[None],
        grad_key[None],
        grad_value[None],
        grad_filter,
        grad_skip,
    )


def solution(mesh):
    return jax.shard_map(
        on_device,
        mesh=mesh,
        in_specs=(
            P("dp", "seq", "chan"),
            P("dp", "seq", "chan"),
            P("dp", "seq", "chan"),
            P("dp", "seq", "chan"),
            P("seq", "chan"),
            P("chan"),
        ),
        out_specs=(
            P("dp", "seq", "chan"),
            P("dp", "seq", "chan"),
            P("dp", "seq", "chan"),
            P("dp", "seq", "chan"),
            P("seq", "chan"),
            P("chan"),
        ),
        check_vma=False,
    )
```

```python
import functools
import math

import jax
import jax.numpy as jnp
import ml_dtypes
import numpy as np
from jax import lax
from jax.experimental import pallas as pl
from jax.experimental.pallas import tpu as pltpu
from jax.sharding import PartitionSpec as P

full_precision = lax.Precision.HIGHEST
MESH = pl.DeviceIdType.MESH
LANES = 128
INNER = 128
ROWS = 16


def transform_tables(seq_length):
    full_size = 2 * seq_length
    outer = full_size // INNER
    firsts = outer // 2
    kept = outer // 2 + 1
    k1 = np.arange(kept)
    n1 = np.arange(firsts)
    first = 2.0 * np.pi * (k1[:, None] * n1[None, :] % outer) / outer
    first_parts = np.stack([np.cos(first), -np.sin(first)], axis=1).reshape(2 * kept, firsts)
    live = np.ones(2 * kept, bool)
    live[[1, 2 * kept - 1]] = False
    enter = np.kron(first_parts[live], np.eye(ROWS))
    weight = np.where((k1 == 0) | (k1 == outer // 2), 1.0, 2.0) / full_size
    leave = np.kron((first_parts.reshape(kept, 2, firsts) * weight[:, None, None]).reshape(2 * kept, firsts)[live].T, np.eye(ROWS))
    n2 = np.arange(INNER)
    k2 = np.arange(INNER)
    freq = k1[:, None, None] + outer * k2[None, :, None]
    angle = 2.0 * np.pi * (freq * n2[None, None, :] % full_size) / full_size
    cos, sin = np.cos(angle), np.sin(angle)
    middle = np.concatenate(
        [np.concatenate([cos, sin], axis=2), np.concatenate([-sin, cos], axis=2)], axis=1
    )
    back = np.transpose(middle, (0, 2, 1))
    return tuple(np.asarray(t).astype(ml_dtypes.bfloat16) for t in (enter, middle, back, leave))


def fused_kernel(
    factor,
    q_hbm, k_hbm, v_hbm, ct_hbm, taps_hbm, skip_ref, enter_ref, middle_ref, back_ref, leave_ref, enter_low_ref, leave_low_ref,
    out_hbm, gq_hbm, gk_hbm, gv_hbm, gf_hbm, gs_ref,
    acts, taps, stage, hstage, xs, ws, hs, cross, scross, spec, ys, cs, ss, gain,
    in_sem, out_sem, x_send, x2_send, w_send, h_send, h2_send, f_send, y_send, c_send, s_send, n_send, g_send,
    x_recv, w_recv, h_recv, cross_recv, scross_recv, y_recv, c_recv, s_recv, g_recv,
):
    z = lax.axis_index("seq")
    b = lax.axis_index("dp")
    seq_count, batch_count = 4, 2
    groups = seq_count * batch_count
    me = z * batch_count + b
    block_count, rows = acts.shape[1], acts.shape[2]
    steps = block_count // batch_count
    per_row = rows // INNER
    act_in = (q_hbm, k_hbm, v_hbm, ct_hbm)
    act_out = (out_hbm, gq_hbm, gk_hbm, gv_hbm)

    def partner(i):
        pz = lax.rem(z + 1 + i // batch_count, seq_count)
        pb = lax.rem(b + 1 + lax.rem(i, batch_count), batch_count)
        return pz, pb, pz * batch_count + pb

    def cols(blk):
        return pl.ds(pl.multiple_of(blk * LANES, LANES), LANES)

    def upper_owner(k):
        return jnp.where(jnp.logical_and(lax.rem(k, 2) == 1, k < 6), 3, 2)

    def merge_order(m):
        order = [0, 2, 4, 6, 1, 3, 5, 7] + list(range(8, steps))
        k = 0
        for i, step in enumerate(order):
            k = k + jnp.where(m == i, step, 0)
        return k

    def input_copies(blk):
        found = [
            pltpu.make_async_copy(act_in[a].at[0, :, cols(blk)], acts.at[a, blk], in_sem.at[a, blk])
            for a in range(4)
        ]
        found.append(pltpu.make_async_copy(taps_hbm.at[:, cols(blk)], taps.at[blk], in_sem.at[4, blk]))
        return found

    def output_copies(blk):
        found = [
            pltpu.make_async_copy(acts.at[a, blk], act_out[a].at[0, :, cols(blk)], out_sem.at[a, blk])
            for a in range(4)
        ]
        found.append(pltpu.make_async_copy(taps.at[blk], gf_hbm.at[:, cols(blk)], out_sem.at[4, blk]))
        return found

    def start_input(blk, carry):
        for copy in input_copies(blk):
            copy.start()
        return carry

    lax.fori_loop(0, block_count, start_input, 0)

    barrier = pltpu.get_barrier_semaphore()

    def greet(i, carry):
        pz, pb, _ = partner(i)
        pl.semaphore_signal(barrier, inc=1, device_id={"seq": pz, "dp": pb}, device_id_type=MESH)
        return carry

    lax.fori_loop(0, groups - 1, greet, 0)
    pl.semaphore_wait(barrier, groups - 1)

    def remote(src, dst, send, recv, pz, pb):
        return pltpu.make_async_remote_copy(
            src_ref=src, dst_ref=dst, send_sem=send, recv_sem=recv,
            device_id={"seq": pz, "dp": pb}, device_id_type=MESH,
        )

    def arrived(ref, sem):
        pltpu.make_async_copy(ref, ref, sem).wait()

    def move(src, dst, send, recv, pz, pb):
        here = jnp.logical_and(pz == z, pb == b)

        @pl.when(here)
        def _():
            pltpu.make_async_copy(src, dst, recv).start()

        @pl.when(jnp.logical_not(here))
        def _():
            remote(src, dst, send, recv, pz, pb).start()

    def settle(src, dst, send, recv, pz, pb):
        @pl.when(jnp.logical_not(jnp.logical_and(pz == z, pb == b)))
        def _():
            arrived(src, send)

    def give_inputs(blk, act):
        k = blk // batch_count
        pb = lax.rem(blk, batch_count)
        owner = upper_owner(k)
        target = jnp.where(z < 2, 1, owner)
        slot = lax.rem(z, 2) * batch_count + b
        act(stage.at[blk, 0], xs.at[k, me], x_send.at[blk], x_recv.at[k, me], target, pb)

        @pl.when(pb == b)
        def _():
            act(hstage.at[k], hs.at[k, z], h_send.at[k], h_recv.at[k, z], target, b)

        act(stage.at[blk, 1], ws.at[k, slot], w_send.at[blk], w_recv.at[k, slot], target, pb)

    def give_across(k, act):
        owner = upper_owner(k)
        for pb in range(batch_count):
            blk = k * batch_count + pb
            act(stage.at[blk, 0], xs.at[k, me], x2_send.at[blk], x_recv.at[k, me], owner, pb)
        act(hstage.at[k], hs.at[k, z], h2_send.at[k], h_recv.at[k, z], owner, b)

    def forward_low(k, act):
        owner = upper_owner(k)
        for bb in range(batch_count):
            act(xs.at[k, bb], xs.at[k, bb], f_send.at[k, bb], x_recv.at[k, bb], owner, b)
        act(hs.at[k, 0], hs.at[k, 0], f_send.at[k, 2], h_recv.at[k, 0], owner, b)

    def give_upper(k, act):
        blk = k * batch_count + b
        for zz in range(2):
            for bb in range(batch_count):
                at = zz * batch_count + bb
                act(xs.at[k, at], cross.at[k, at], c_send.at[k, at], cross_recv.at[k, at], 1, b)
            act(hs.at[k, zz], scross.at[k, zz], s_send.at[k, zz], scross_recv.at[k, zz], 1, b)
        for zz in range(2, 4):
            for bb in range(batch_count):
                at = zz * batch_count + bb
                low = at - 2 * batch_count
                act(ws.at[k, low], ys.at[blk], y_send.at[k, low], y_recv.at[blk], zz, bb)
                act(xs.at[k, at], cs.at[blk], c_send.at[k, at], c_recv.at[blk], zz, bb)
            act(hs.at[k, zz], ss.at[blk], s_send.at[k, zz], s_recv.at[blk], zz, b)

    def give_low_conv(k, act):
        blk = k * batch_count + b
        for zz in range(2):
            for bb in range(batch_count):
                at = zz * batch_count + bb
                act(ws.at[k, at], ys.at[blk], y_send.at[k, at], y_recv.at[blk], zz, bb)

    def give_low_corr(k, act):
        blk = k * batch_count + b
        for zz in range(2):
            for bb in range(batch_count):
                at = zz * batch_count + bb
                act(xs.at[k, 4 + at], cs.at[blk], c_send.at[k, at], c_recv.at[blk], zz, bb)
            act(hs.at[k, 2 + zz], ss.at[blk], s_send.at[k, zz], s_recv.at[blk], zz, b)

    ahead = 2

    def send_block(blk, carry):
        for copy in input_copies(blk):
            copy.wait()
        mixed = (acts[1, blk].astype(jnp.float32) * acts[2, blk].astype(jnp.float32)).astype(jnp.bfloat16)
        weighted = (acts[3, blk].astype(jnp.float32) * acts[0, blk].astype(jnp.float32)).astype(jnp.bfloat16)
        stage[blk, 0] = mixed
        stage[blk, 1] = weighted
        gain[me, pl.ds(blk, 1), :] = jnp.sum(
            weighted.astype(jnp.float32) * mixed.astype(jnp.float32), axis=0, keepdims=True
        )

        @pl.when(lax.rem(blk, batch_count) == b)
        def _():
            hstage[blk // batch_count] = taps[blk].astype(jnp.bfloat16)

        give_inputs(blk, move)

        @pl.when(jnp.logical_and(z == 1, jnp.logical_and(lax.rem(blk, 2) == 1, blk < 2 * ahead)))
        def _():
            give_across(blk // batch_count, move)

        return carry

    lax.fori_loop(0, block_count, send_block, 0)

    def send_gain(i, carry):
        pz, pb, idx = partner(i)
        remote(gain.at[me], gain.at[me], g_send.at[idx], g_recv.at[me], pz, pb).start()
        return carry

    lax.fori_loop(0, groups - 1, send_gain, 0)

    def transform(k, low):
        kept = (middle_ref.shape[0] + 1) // 2 if low else middle_ref.shape[0]
        firsts = (2 if low else 4) * per_row
        enter_table = enter_low_ref if low else enter_ref
        leave_table = leave_low_ref if low else leave_ref
        scale = 2 if low else 1
        live = [(k1, part) for k1 in range(kept) for part in range(2) if part == 0 or 0 < k1 < kept - 1]
        for k1 in (0, kept - 1):
            spec[k1, INNER:, :] = jnp.zeros((INNER, spec.shape[2]), jnp.bfloat16)

        def enter(g, inner):
            def piece(ref):
                return jnp.concatenate(
                    [
                        ref(n1 // per_row, pl.ds(pl.multiple_of(n1 % per_row * INNER + g * ROWS, ROWS), ROWS))
                        for n1 in range(firsts)
                    ],
                    axis=0,
                )

            def weighted_rows(s, r, bb):
                if low:
                    return ws[k, s * batch_count + bb, r, :]
                if s < 2:
                    return jnp.zeros((ROWS, LANES), jnp.bfloat16)
                return ws[k, (s - 2) * batch_count + bb, r, :]

            signals = [
                piece(lambda s, r, bb=bb: xs[k, s * batch_count + bb, r, :]) for bb in range(batch_count)
            ]
            signals += [piece(lambda s, r, bb=bb: weighted_rows(s, r, bb)) for bb in range(batch_count)]
            signals.append(piece(lambda s, r: hs[k, s, r, :]))
            stacked = jnp.concatenate(signals, axis=1)
            grid = jnp.dot(enter_table[...], stacked, preferred_element_type=jnp.float32).astype(jnp.bfloat16)
            for i, (k1, part) in enumerate(live):
                at = i * ROWS
                spec[k1, pl.ds(pl.multiple_of(part * INNER + g * ROWS, ROWS), ROWS), :] = grid[at : at + ROWS]
            return inner

        lax.fori_loop(0, INNER // ROWS, enter, 0)

        def products(full):
            real, imag = full[:INNER], full[INNER:]

            def take(i):
                return real[:, i * LANES : (i + 1) * LANES], imag[:, i * LANES : (i + 1) * LANES]

            hr, hi = take(2 * batch_count)
            out_real, out_imag = [], []
            for bb in range(batch_count):
                mr, mi = take(bb)
                out_real.append(mr * hr - mi * hi)
                out_imag.append(mr * hi + mi * hr)
            for bb in range(batch_count):
                wr, wi = take(batch_count + bb)
                out_real.append(hr * wr + hi * wi)
                out_imag.append(hr * wi - hi * wr)
            slope_real, slope_imag = 0.0, 0.0
            for bb in range(batch_count):
                mr, mi = take(bb)
                wr, wi = take(batch_count + bb)
                slope_real = slope_real + (mr * wr + mi * wi)
                slope_imag = slope_imag + (mr * wi - mi * wr)
            out_real.append(slope_real)
            out_imag.append(slope_imag)
            return jnp.concatenate(
                [
                    jnp.concatenate([t.astype(jnp.bfloat16) for t in out_real], axis=1),
                    jnp.concatenate([t.astype(jnp.bfloat16) for t in out_imag], axis=1),
                ],
                axis=0,
            )

        def middle(firsts_now):
            fulls = [
                jnp.dot(middle_ref[scale * k1], spec[k1], preferred_element_type=jnp.float32) for k1 in firsts_now
            ]
            turned = [products(full) for full in fulls]
            backs = [
                jnp.dot(back_ref[scale * k1], turn, preferred_element_type=jnp.float32).astype(jnp.bfloat16)
                for k1, turn in zip(firsts_now, turned)
            ]
            for k1, back in zip(firsts_now, backs):
                spec[k1] = back

        def middle_pair(p, inner):
            middle([2 * p, 2 * p + 1])
            return inner

        lax.fori_loop(0, kept // 2, middle_pair, 0)
        middle([kept - 1])

        def leave(g, inner):
            stacked = jnp.concatenate(
                [
                    spec[k1, pl.ds(pl.multiple_of(part * INNER + g * ROWS, ROWS), ROWS), :]
                    for k1, part in live
                ],
                axis=0,
            )
            grid = jnp.dot(leave_table[...], stacked, preferred_element_type=jnp.float32).astype(jnp.bfloat16)
            for n1 in range(firsts):
                s = n1 // per_row
                r = pl.ds(pl.multiple_of(n1 % per_row * INNER + g * ROWS, ROWS), ROWS)
                part = grid[n1 * ROWS : (n1 + 1) * ROWS]
                for bb in range(batch_count):
                    if low:
                        ws[k, s * batch_count + bb, r, :] = part[:, bb * LANES : (bb + 1) * LANES]
                    elif s >= 2:
                        ws[k, (s - 2) * batch_count + bb, r, :] = part[:, bb * LANES : (bb + 1) * LANES]
                    at = batch_count + bb
                    to = s * batch_count + bb + (4 if low else 0)
                    xs[k, to, r, :] = part[:, at * LANES : (at + 1) * LANES]
                hs[k, s + (2 if low else 0), r, :] = part[:, 2 * batch_count * LANES :]
            return inner

        lax.fori_loop(0, INNER // ROWS, leave, 0)

    def merge_low(k):
        for zz in range(2):
            for bb in range(batch_count):
                at = zz * batch_count + bb
                arrived(cross.at[k, at], cross_recv.at[k, at])
                xs[k, 4 + at] = (
                    xs[k, 4 + at].astype(jnp.float32) + cross[k, at].astype(jnp.float32)
                ).astype(jnp.bfloat16)
            arrived(scross.at[k, zz], scross_recv.at[k, zz])
            hs[k, 2 + zz] = (
                hs[k, 2 + zz].astype(jnp.float32) + scross[k, zz].astype(jnp.float32)
            ).astype(jnp.bfloat16)
        give_low_corr(k, move)

    def finish_block(blk, carry):
        k = blk // batch_count
        pb = lax.rem(blk, batch_count)
        arrived(ys.at[blk], y_recv.at[blk])
        arrived(cs.at[blk], c_recv.at[blk])
        query = acts[0, blk].astype(jnp.float32)
        key = acts[1, blk].astype(jnp.float32)
        value = acts[2, blk].astype(jnp.float32)
        cot = acts[3, blk].astype(jnp.float32)
        skip = skip_ref[pl.ds(blk, 1), :]
        signal = ys[blk].astype(jnp.float32) + skip * stage[blk, 0].astype(jnp.float32)
        back = cs[blk].astype(jnp.float32) + skip * stage[blk, 1].astype(jnp.float32)
        acts[0, blk] = (query * signal).astype(jnp.bfloat16)
        acts[1, blk] = (cot * signal).astype(jnp.bfloat16)
        acts[2, blk] = (back * value).astype(jnp.bfloat16)
        acts[3, blk] = (back * key).astype(jnp.bfloat16)
        copies = output_copies(blk)
        for copy in copies[:4]:
            copy.start()
        arrived(ss.at[blk], s_recv.at[blk])

        @pl.when(pb == b)
        def _():
            remote(ss.at[blk], ss.at[blk], n_send.at[k], s_recv.at[blk], z, 1 - b).start()

        taps[blk] = factor * ss[blk].astype(jnp.float32)
        copies[4].start()
        return carry

    def finish_step(k):
        for bb in range(batch_count):
            finish_block(k * batch_count + lax.rem(b + bb, batch_count), 0)

    def finish_rest(m, carry):
        finish_step(merge_order(m))
        return carry

    lag = 5
    wait_upper = 4

    @pl.when(z == 0)
    def _():
        lax.fori_loop(0, steps, finish_rest, 0)

    @pl.when(z == 1)
    def _():
        def step(k, carry):
            @pl.when(k < steps)
            def _():
                for s in range(4):
                    arrived(xs.at[k, s], x_recv.at[k, s])
                for s in range(2):
                    arrived(hs.at[k, s], h_recv.at[k, s])
                forward_low(k, move)

                @pl.when(k < steps - ahead)
                def _():
                    give_across(k + ahead, move)

                for s in range(4):
                    arrived(ws.at[k, s], w_recv.at[k, s])
                transform(k, True)
                give_low_conv(k, move)

            @pl.when(k >= lag)
            def _():
                merge_low(merge_order(k - lag))

            @pl.when(k >= lag + 1)
            def _():
                finish_step(merge_order(k - lag - 1))

            return carry

        lax.fori_loop(0, steps + lag, step, 0)
        finish_step(merge_order(steps - 1))

    @pl.when(z >= 2)
    def _():
        def step(k, carry):
            @pl.when(upper_owner(k) == z)
            def _():
                for s in range(8):
                    arrived(xs.at[k, s], x_recv.at[k, s])
                for s in range(4):
                    arrived(hs.at[k, s], h_recv.at[k, s])
                    arrived(ws.at[k, s], w_recv.at[k, s])
                transform(k, False)
                give_upper(k, move)

            @pl.when(k >= wait_upper)
            def _():
                finish_step(merge_order(k - wait_upper))

            return carry

        lax.fori_loop(0, steps, step, 0)

        def rest(m, carry):
            finish_step(merge_order(m))
            return carry

        lax.fori_loop(steps - wait_upper, steps, rest, 0)

    def wait_gain(i, carry):
        _, _, idx = partner(i)
        arrived(gain.at[idx], g_recv.at[idx])
        arrived(gain.at[me], g_send.at[idx])
        return carry

    lax.fori_loop(0, groups - 1, wait_gain, 0)
    total = gain[0]
    for s in range(1, groups):
        total = total + gain[s]
    gs_ref[...] = factor * total

    def drain(blk, carry):
        for copy in output_copies(blk):
            copy.wait()
        give_inputs(blk, settle)
        k = blk // batch_count

        @pl.when(lax.rem(blk, batch_count) == b)
        def _():
            arrived(ss.at[blk], n_send.at[k])

            @pl.when(z == 1)
            def _():
                give_across(k, settle)
                forward_low(k, settle)
                give_low_conv(k, settle)
                give_low_corr(k, settle)

            @pl.when(upper_owner(k) == z)
            def _():
                give_upper(k, settle)

        return carry

    lax.fori_loop(0, block_count, drain, 0)


def fused(query_proj, key_proj, value_proj, cotangent, long_filter, skip_gain):
    rows, width = query_proj.shape[1:]
    seq_count = lax.axis_size("seq")
    batch_count = lax.axis_size("dp")
    groups = seq_count * batch_count
    seq_length = seq_count * rows
    block_count = width // LANES
    steps = block_count // batch_count
    factor = (batch_count * seq_length) ** (-0.5)
    tables = transform_tables(seq_length)
    low_tables = transform_tables(seq_length // 2)
    tables = tables + (low_tables[0], low_tables[3])
    kept = tables[1].shape[0]
    signals = 2 * batch_count + 1
    half = jnp.bfloat16
    dma = pltpu.SemaphoreType.DMA
    hbm = pl.BlockSpec(memory_space=pl.ANY)
    vmem = pl.BlockSpec(memory_space=pltpu.VMEM)
    flops = 2 * steps * signals * LANES * (2 * tables[0].size * INNER // ROWS + 2 * tables[1].size)
    results = pl.pallas_call(
        functools.partial(fused_kernel, factor),
        out_shape=[jax.ShapeDtypeStruct((1, rows, width), half)] * 4
        + [
            jax.ShapeDtypeStruct((rows, width), jnp.float32),
            jax.ShapeDtypeStruct((block_count, LANES), jnp.float32),
        ],
        in_specs=[hbm] * 5 + [vmem] * 7,
        out_specs=[hbm] * 5 + [vmem],
        scratch_shapes=[
            pltpu.VMEM((4, block_count, rows, LANES), half),
            pltpu.VMEM((block_count, rows, LANES), jnp.float32),
            pltpu.VMEM((block_count, 2, rows, LANES), half),
            pltpu.VMEM((steps, rows, LANES), half),
            pltpu.VMEM((steps, groups, rows, LANES), half),
            pltpu.VMEM((steps, groups // 2, rows, LANES), half),
            pltpu.VMEM((steps, seq_count, rows, LANES), half),
            pltpu.VMEM((steps, groups // 2, rows, LANES), half),
            pltpu.VMEM((steps, seq_count // 2, rows, LANES), half),
            pltpu.VMEM((kept, 2 * INNER, signals * LANES), half),
            pltpu.VMEM((block_count, rows, LANES), half),
            pltpu.VMEM((block_count, rows, LANES), half),
            pltpu.VMEM((block_count, rows, LANES), half),
            pltpu.VMEM((groups, block_count, LANES), jnp.float32),
            dma((5, block_count)),
            dma((5, block_count)),
            dma((block_count,)),
            dma((block_count,)),
            dma((block_count,)),
            dma((steps,)),
            dma((steps,)),
            dma((steps, 3)),
            dma((steps, groups // 2)),
            dma((steps, groups)),
            dma((steps, seq_count)),
            dma((steps,)),
            dma((groups,)),
            dma((steps, groups)),
            dma((steps, groups // 2)),
            dma((steps, seq_count)),
            dma((steps, groups // 2)),
            dma((steps, seq_count // 2)),
            dma((block_count,)),
            dma((block_count,)),
            dma((block_count,)),
            dma((groups,)),
        ],
        compiler_params=pltpu.CompilerParams(
            collective_id=0, has_side_effects=True, vmem_limit_bytes=62 * 1024 * 1024
        ),
        cost_estimate=pl.CostEstimate(
            flops=flops, bytes_accessed=24 * rows * width, transcendentals=0
        ),
    )(
        query_proj, key_proj, value_proj, cotangent, long_filter,
        skip_gain.reshape(block_count, LANES), *(jnp.asarray(t) for t in tables),
    )
    return tuple(results[:5]) + (results[5].reshape(width),)


def dft_tables(seq_length):
    full_size = 2 * seq_length
    inner_size = 128
    outer_size = full_size // inner_size
    half_size = outer_size // 2
    outer_index = jnp.arange(outer_size, dtype=jnp.int32)
    half_index = jnp.arange(half_size, dtype=jnp.int32)
    inner_index = jnp.arange(inner_size, dtype=jnp.int32)
    first_angle = (
        2.0
        * math.pi
        / outer_size
        * (outer_index[:, None] * half_index[None, :] % outer_size).astype(jnp.float32)
    )
    twist_angle = (
        2.0
        * math.pi
        / full_size
        * (outer_index[:, None] * inner_index[None, :] % full_size).astype(jnp.float32)
    )
    last_angle = (
        2.0
        * math.pi
        / inner_size
        * (inner_index[:, None] * inner_index[None, :] % inner_size).astype(jnp.float32)
    )
    return (
        jnp.cos(first_angle),
        jnp.sin(first_angle),
        jnp.cos(twist_angle),
        jnp.sin(twist_angle),
        jnp.cos(last_angle),
        jnp.sin(last_angle),
    )


def forward(signal, tables):
    cos_first, sin_first, cos_twist, sin_twist, cos_last, sin_last = tables
    half_size = cos_first.shape[1]
    signal_grid = signal.reshape(signal.shape[0], half_size, 128)
    real_first = jnp.einsum("kn,rnm->rkm", cos_first, signal_grid, precision=full_precision)
    imag_first = -jnp.einsum("kn,rnm->rkm", sin_first, signal_grid, precision=full_precision)
    real_twist = real_first * cos_twist + imag_first * sin_twist
    imag_twist = imag_first * cos_twist - real_first * sin_twist
    real_last = jnp.einsum(
        "rkm,mj->rkj", real_twist, cos_last, precision=full_precision
    ) + jnp.einsum("rkm,mj->rkj", imag_twist, sin_last, precision=full_precision)
    imag_last = jnp.einsum(
        "rkm,mj->rkj", imag_twist, cos_last, precision=full_precision
    ) - jnp.einsum("rkm,mj->rkj", real_twist, sin_last, precision=full_precision)
    return (real_last, imag_last)


def inverse(real_part, imag_part, tables):
    cos_first, sin_first, cos_twist, sin_twist, cos_last, sin_last = tables
    half_size = cos_first.shape[1]
    row_total = real_part.shape[0]
    real_inner = jnp.einsum(
        "rkj,jm->rkm", real_part, cos_last, precision=full_precision
    ) - jnp.einsum("rkj,jm->rkm", imag_part, sin_last, precision=full_precision)
    imag_inner = jnp.einsum(
        "rkj,jm->rkm", imag_part, cos_last, precision=full_precision
    ) + jnp.einsum("rkj,jm->rkm", real_part, sin_last, precision=full_precision)
    real_twist = real_inner * cos_twist - imag_inner * sin_twist
    imag_twist = imag_inner * cos_twist + real_inner * sin_twist
    result = jnp.einsum(
        "kn,rkm->rnm", cos_first, real_twist, precision=full_precision
    ) - jnp.einsum("kn,rkm->rnm", sin_first, imag_twist, precision=full_precision)
    return (result / (2.0 * half_size * 128)).reshape(row_total, half_size * 128)


def filter_block(items, tables):
    mixed_blk, weighted_blk, kernel = items
    batches, chan_width, seq_length = mixed_blk.shape
    row_count = batches * chan_width
    mixed_wide = mixed_blk.astype(jnp.float32)
    weighted_wide = weighted_blk.astype(jnp.float32)
    stacked = jnp.concatenate(
        [
            mixed_wide.reshape(row_count, seq_length),
            weighted_wide.reshape(row_count, seq_length),
            kernel,
        ],
        axis=0,
    )
    real_spec, imag_spec = forward(stacked, tables)
    grid_shape = real_spec.shape[1:]
    mixed_real = real_spec[:row_count].reshape((batches, chan_width) + grid_shape)
    mixed_imag = imag_spec[:row_count].reshape((batches, chan_width) + grid_shape)
    weighted_real = real_spec[row_count : 2 * row_count].reshape((batches, chan_width) + grid_shape)
    weighted_imag = imag_spec[row_count : 2 * row_count].reshape((batches, chan_width) + grid_shape)
    kernel_real = real_spec[2 * row_count :][None]
    kernel_imag = imag_spec[2 * row_count :][None]
    conv_real = mixed_real * kernel_real - mixed_imag * kernel_imag
    conv_imag = mixed_real * kernel_imag + mixed_imag * kernel_real
    corr_real = kernel_real * weighted_real + kernel_imag * weighted_imag
    corr_imag = kernel_real * weighted_imag - kernel_imag * weighted_real
    slope_real = jnp.sum(mixed_real * weighted_real + mixed_imag * weighted_imag, axis=0)
    slope_imag = jnp.sum(mixed_real * weighted_imag - mixed_imag * weighted_real, axis=0)
    spec_real = jnp.concatenate(
        [
            conv_real.reshape((row_count,) + grid_shape),
            corr_real.reshape((row_count,) + grid_shape),
            slope_real,
        ],
        axis=0,
    )
    spec_imag = jnp.concatenate(
        [
            conv_imag.reshape((row_count,) + grid_shape),
            corr_imag.reshape((row_count,) + grid_shape),
            slope_imag,
        ],
        axis=0,
    )
    result = inverse(spec_real, spec_imag, tables)
    conv_vals = result[:row_count].reshape(batches, chan_width, seq_length).astype(jnp.bfloat16)
    corr_vals = (
        result[row_count : 2 * row_count]
        .reshape(batches, chan_width, seq_length)
        .astype(jnp.bfloat16)
    )
    slope = result[2 * row_count :]
    return (conv_vals, corr_vals, slope)


def run_blocks(mixed_rows, weighted_rows, filter_part):
    batches, part_width, seq_length = mixed_rows.shape
    block_width = min(part_width, 8)
    block_count = part_width // block_width
    tables = dft_tables(seq_length)

    def stack_rows(arr):
        return jnp.moveaxis(arr.reshape(batches, block_count, block_width, seq_length), 1, 0)

    def unstack_rows(arr):
        return jnp.moveaxis(arr, 0, 1).reshape(batches, part_width, seq_length)

    def one_block(items):
        return filter_block(items, tables)

    items = (
        stack_rows(mixed_rows),
        stack_rows(weighted_rows),
        filter_part.reshape(block_count, block_width, seq_length),
    )
    conv_vals, corr_vals, slope = lax.map(one_block, items)
    return (unstack_rows(conv_vals), unstack_rows(corr_vals), slope.reshape(part_width, seq_length))


def on_device(query_proj, key_proj, value_proj, cotangent, long_filter, skip_gain):
    rows, width = query_proj.shape[1:]
    grouped = lax.axis_size("seq") == 4 and lax.axis_size("dp") == 2
    if grouped and rows % INNER == 0 and width >= 16 * LANES and width % (2 * LANES) == 0 and rows * width <= 2**20:
        return fused(query_proj, key_proj, value_proj, cotangent, long_filter, skip_gain)
    return spread(query_proj, key_proj, value_proj, cotangent, long_filter, skip_gain)


def spread(query_proj, key_proj, value_proj, cotangent, long_filter, skip_gain):
    query_rows = query_proj[0].astype(jnp.float32)
    key_rows = key_proj[0].astype(jnp.float32)
    value_rows = value_proj[0].astype(jnp.float32)
    cot_rows = cotangent[0].astype(jnp.float32)
    local_length = query_proj.shape[1]
    chan_width = query_proj.shape[2]
    seq_count = lax.axis_size("seq")
    batch_count = lax.axis_size("dp")
    factor = (batch_count * seq_count * local_length) ** (-0.5)
    mixed = (key_rows * value_rows).astype(jnp.bfloat16)
    weighted = (cot_rows * query_rows).astype(jnp.bfloat16)
    mixed_wide = mixed.astype(jnp.float32)
    weighted_wide = weighted.astype(jnp.float32)
    gain_term = factor * jnp.sum(weighted_wide * mixed_wide, axis=0)
    grad_skip = lax.psum(gain_term, ("seq", "dp"))
    filter_share = lax.all_to_all(long_filter.T, "seq", split_axis=0, concat_axis=1, tiled=True)
    groups = seq_count * batch_count
    share_width = chan_width // groups
    mixed_cols, weighted_cols = (
        lax.all_to_all(mixed.T, ("seq", "dp"), split_axis=0, concat_axis=1, tiled=True),
        lax.all_to_all(weighted.T, ("seq", "dp"), split_axis=0, concat_axis=1, tiled=True),
    )

    def to_sequences(arr):
        arr = arr.reshape(share_width, seq_count, batch_count, local_length)
        return jnp.transpose(arr, (2, 0, 1, 3)).reshape(
            batch_count, share_width, seq_count * local_length
        )

    def to_pieces(arr):
        arr = arr.reshape(batch_count, share_width, seq_count, local_length)
        return jnp.transpose(arr, (1, 2, 0, 3)).reshape(share_width, groups * local_length)

    filter_part = lax.dynamic_slice_in_dim(
        filter_share, lax.axis_index("dp") * share_width, share_width, 0
    )
    conv_vals, corr_vals, slope = run_blocks(
        to_sequences(mixed_cols), to_sequences(weighted_cols), filter_part
    )
    conv_back, corr_back = (
        lax.all_to_all(
            to_pieces(conv_vals), ("seq", "dp"), split_axis=1, concat_axis=0, tiled=True
        ),
        lax.all_to_all(
            to_pieces(corr_vals), ("seq", "dp"), split_axis=1, concat_axis=0, tiled=True
        ),
    )
    slope_share = lax.all_gather(slope, "dp", axis=0, tiled=True)
    slope_rows = lax.all_to_all(slope_share, "seq", split_axis=1, concat_axis=0, tiled=True)
    grad_filter = factor * slope_rows.T
    conv_rows = conv_back.T.astype(jnp.float32)
    corr_rows = corr_back.T.astype(jnp.float32)
    signal = conv_rows + skip_gain[None, :] * mixed_wide
    output = (query_rows * signal).astype(jnp.bfloat16)
    grad_query = (cot_rows * signal).astype(jnp.bfloat16)
    back = corr_rows + skip_gain[None, :] * weighted_wide
    grad_key = (back * value_rows).astype(jnp.bfloat16)
    grad_value = (back * key_rows).astype(jnp.bfloat16)
    return (
        output[None],
        grad_query[None],
        grad_key[None],
        grad_value[None],
        grad_filter,
        grad_skip,
    )


def solution(mesh):
    return jax.shard_map(
        on_device,
        mesh=mesh,
        in_specs=(
            P("dp", "seq", "chan"),
            P("dp", "seq", "chan"),
            P("dp", "seq", "chan"),
            P("dp", "seq", "chan"),
            P("seq", "chan"),
            P("chan"),
        ),
        out_specs=(
            P("dp", "seq", "chan"),
            P("dp", "seq", "chan"),
            P("dp", "seq", "chan"),
            P("dp", "seq", "chan"),
            P("seq", "chan"),
            P("chan"),
        ),
        check_vma=False,
    )
```

```python
import functools
import math

import jax
import jax.numpy as jnp
import ml_dtypes
import numpy as np
from jax import lax
from jax.experimental import pallas as pl
from jax.experimental.pallas import tpu as pltpu
from jax.sharding import PartitionSpec as P

full_precision = lax.Precision.HIGHEST
MESH = pl.DeviceIdType.MESH
LANES = 128
INNER = 128
ROWS = 16


def transform_tables(seq_length):
    full_size = 2 * seq_length
    outer = full_size // INNER
    firsts = outer // 2
    kept = outer // 2 + 1
    k1 = np.arange(kept)
    n1 = np.arange(firsts)
    first = 2.0 * np.pi * (k1[:, None] * n1[None, :] % outer) / outer
    first_parts = np.stack([np.cos(first), -np.sin(first)], axis=1).reshape(2 * kept, firsts)
    live = np.ones(2 * kept, bool)
    live[[1, 2 * kept - 1]] = False
    enter = np.kron(first_parts[live], np.eye(ROWS))
    weight = np.where((k1 == 0) | (k1 == outer // 2), 1.0, 2.0) / full_size
    leave = np.kron((first_parts.reshape(kept, 2, firsts) * weight[:, None, None]).reshape(2 * kept, firsts)[live].T, np.eye(ROWS))
    n2 = np.arange(INNER)
    k2 = np.arange(INNER)
    freq = k1[:, None, None] + outer * k2[None, :, None]
    angle = 2.0 * np.pi * (freq * n2[None, None, :] % full_size) / full_size
    cos, sin = np.cos(angle), np.sin(angle)
    middle = np.concatenate(
        [np.concatenate([cos, sin], axis=2), np.concatenate([-sin, cos], axis=2)], axis=1
    )
    back = np.transpose(middle, (0, 2, 1))
    return tuple(np.asarray(t).astype(ml_dtypes.bfloat16) for t in (enter, middle, back, leave))


def fused_kernel(
    factor,
    q_hbm, k_hbm, v_hbm, ct_hbm, taps_hbm, skip_ref, enter_ref, middle_ref, back_ref, leave_ref, enter_low_ref, leave_low_ref,
    out_hbm, gq_hbm, gk_hbm, gv_hbm, gf_hbm, gs_ref,
    acts, taps, stage, hstage, xs, ws, hs, cross, scross, spec, ys, cs, ss, gain,
    in_sem, out_sem, x_send, x2_send, w_send, h_send, h2_send, f_send, y_send, c_send, s_send, n_send, g_send,
    x_recv, w_recv, h_recv, cross_recv, scross_recv, y_recv, c_recv, s_recv, g_recv,
):
    z = lax.axis_index("seq")
    b = lax.axis_index("dp")
    seq_count, batch_count = 4, 2
    groups = seq_count * batch_count
    me = z * batch_count + b
    block_count, rows = acts.shape[1], acts.shape[2]
    steps = block_count // batch_count
    per_row = rows // INNER
    act_in = (q_hbm, k_hbm, v_hbm, ct_hbm)
    act_out = (out_hbm, gq_hbm, gk_hbm, gv_hbm)

    def partner(i):
        pz = lax.rem(z + 1 + i // batch_count, seq_count)
        pb = lax.rem(b + 1 + lax.rem(i, batch_count), batch_count)
        return pz, pb, pz * batch_count + pb

    def cols(blk):
        return pl.ds(pl.multiple_of(blk * LANES, LANES), LANES)

    def upper_owner(k):
        return jnp.where(k == 1, 3, 2)

    def merge_order(m):
        order = [0, 2, 3, 4, 1] + list(range(5, steps))
        k = 0
        for i, step in enumerate(order):
            k = k + jnp.where(m == i, step, 0)
        return k

    def input_copies(blk):
        found = [
            pltpu.make_async_copy(act_in[a].at[0, :, cols(blk)], acts.at[a, blk], in_sem.at[a, blk])
            for a in range(4)
        ]
        found.append(pltpu.make_async_copy(taps_hbm.at[:, cols(blk)], taps.at[blk], in_sem.at[4, blk]))
        return found

    def output_copies(blk):
        found = [
            pltpu.make_async_copy(acts.at[a, blk], act_out[a].at[0, :, cols(blk)], out_sem.at[a, blk])
            for a in range(4)
        ]
        found.append(pltpu.make_async_copy(taps.at[blk], gf_hbm.at[:, cols(blk)], out_sem.at[4, blk]))
        return found

    def start_input(blk, carry):
        for copy in input_copies(blk):
            copy.start()
        return carry

    lax.fori_loop(0, block_count, start_input, 0)

    barrier = pltpu.get_barrier_semaphore()

    def greet(i, carry):
        pz, pb, _ = partner(i)
        pl.semaphore_signal(barrier, inc=1, device_id={"seq": pz, "dp": pb}, device_id_type=MESH)
        return carry

    lax.fori_loop(0, groups - 1, greet, 0)
    pl.semaphore_wait(barrier, groups - 1)

    def remote(src, dst, send, recv, pz, pb):
        return pltpu.make_async_remote_copy(
            src_ref=src, dst_ref=dst, send_sem=send, recv_sem=recv,
            device_id={"seq": pz, "dp": pb}, device_id_type=MESH,
        )

    def arrived(ref, sem):
        pltpu.make_async_copy(ref, ref, sem).wait()

    def move(src, dst, send, recv, pz, pb):
        here = jnp.logical_and(pz == z, pb == b)

        @pl.when(here)
        def _():
            pltpu.make_async_copy(src, dst, recv).start()

        @pl.when(jnp.logical_not(here))
        def _():
            remote(src, dst, send, recv, pz, pb).start()

    def settle(src, dst, send, recv, pz, pb):
        @pl.when(jnp.logical_not(jnp.logical_and(pz == z, pb == b)))
        def _():
            arrived(src, send)

    def give_inputs(blk, act):
        k = blk // batch_count
        pb = lax.rem(blk, batch_count)
        owner = upper_owner(k)
        target = jnp.where(z < 2, 1, owner)
        slot = lax.rem(z, 2) * batch_count + b
        act(stage.at[blk, 0], xs.at[k, me], x_send.at[blk], x_recv.at[k, me], target, pb)

        @pl.when(pb == b)
        def _():
            act(hstage.at[k], hs.at[k, z], h_send.at[k], h_recv.at[k, z], target, b)

        act(stage.at[blk, 1], ws.at[k, slot], w_send.at[blk], w_recv.at[k, slot], target, pb)

    def give_across(k, act):
        owner = upper_owner(k)
        for pb in range(batch_count):
            blk = k * batch_count + pb
            act(stage.at[blk, 0], xs.at[k, me], x2_send.at[blk], x_recv.at[k, me], owner, pb)
        act(hstage.at[k], hs.at[k, z], h2_send.at[k], h_recv.at[k, z], owner, b)

    def forward_low(k, act):
        owner = upper_owner(k)
        for bb in range(batch_count):
            act(xs.at[k, bb], xs.at[k, bb], f_send.at[k, bb], x_recv.at[k, bb], owner, b)
        act(hs.at[k, 0], hs.at[k, 0], f_send.at[k, 2], h_recv.at[k, 0], owner, b)

    def give_upper(k, act):
        blk = k * batch_count + b
        for zz in range(2):
            for bb in range(batch_count):
                at = zz * batch_count + bb
                act(xs.at[k, at], cross.at[k, at], c_send.at[k, at], cross_recv.at[k, at], 1, b)
            act(hs.at[k, zz], scross.at[k, zz], s_send.at[k, zz], scross_recv.at[k, zz], 1, b)
        for zz in range(2, 4):
            for bb in range(batch_count):
                at = zz * batch_count + bb
                low = at - 2 * batch_count
                act(ws.at[k, low], ys.at[blk], y_send.at[k, low], y_recv.at[blk], zz, bb)
                act(xs.at[k, at], cs.at[blk], c_send.at[k, at], c_recv.at[blk], zz, bb)
            act(hs.at[k, zz], ss.at[blk], s_send.at[k, zz], s_recv.at[blk], zz, b)

    def give_low_conv(k, act):
        blk = k * batch_count + b
        for zz in range(2):
            for bb in range(batch_count):
                at = zz * batch_count + bb
                act(ws.at[k, at], ys.at[blk], y_send.at[k, at], y_recv.at[blk], zz, bb)

    def give_low_corr(k, act):
        blk = k * batch_count + b
        for zz in range(2):
            for bb in range(batch_count):
                at = zz * batch_count + bb
                act(xs.at[k, 4 + at], cs.at[blk], c_send.at[k, at], c_recv.at[blk], zz, bb)
            act(hs.at[k, 2 + zz], ss.at[blk], s_send.at[k, zz], s_recv.at[blk], zz, b)

    ahead = 2

    def send_block(blk, carry):
        for copy in input_copies(blk):
            copy.wait()
        mixed = (acts[1, blk].astype(jnp.float32) * acts[2, blk].astype(jnp.float32)).astype(jnp.bfloat16)
        weighted = (acts[3, blk].astype(jnp.float32) * acts[0, blk].astype(jnp.float32)).astype(jnp.bfloat16)
        stage[blk, 0] = mixed
        stage[blk, 1] = weighted
        gain[me, pl.ds(blk, 1), :] = jnp.sum(
            weighted.astype(jnp.float32) * mixed.astype(jnp.float32), axis=0, keepdims=True
        )

        @pl.when(lax.rem(blk, batch_count) == b)
        def _():
            hstage[blk // batch_count] = taps[blk].astype(jnp.bfloat16)

        give_inputs(blk, move)

        @pl.when(jnp.logical_and(z == 1, jnp.logical_and(lax.rem(blk, 2) == 1, blk < 2 * ahead)))
        def _():
            give_across(blk // batch_count, move)

        return carry

    lax.fori_loop(0, block_count, send_block, 0)

    def send_gain(i, carry):
        pz, pb, idx = partner(i)
        remote(gain.at[me], gain.at[me], g_send.at[idx], g_recv.at[me], pz, pb).start()
        return carry

    lax.fori_loop(0, groups - 1, send_gain, 0)

    def transform(k, low):
        kept = (middle_ref.shape[0] + 1) // 2 if low else middle_ref.shape[0]
        firsts = (2 if low else 4) * per_row
        enter_table = enter_low_ref if low else enter_ref
        leave_table = leave_low_ref if low else leave_ref
        scale = 2 if low else 1
        live = [(k1, part) for k1 in range(kept) for part in range(2) if part == 0 or 0 < k1 < kept - 1]
        for k1 in (0, kept - 1):
            spec[k1, INNER:, :] = jnp.zeros((INNER, spec.shape[2]), jnp.bfloat16)

        def enter(g, inner):
            def piece(ref):
                return jnp.concatenate(
                    [
                        ref(n1 // per_row, pl.ds(pl.multiple_of(n1 % per_row * INNER + g * ROWS, ROWS), ROWS))
                        for n1 in range(firsts)
                    ],
                    axis=0,
                )

            def weighted_rows(s, r, bb):
                if low:
                    return ws[k, s * batch_count + bb, r, :]
                if s < 2:
                    return jnp.zeros((ROWS, LANES), jnp.bfloat16)
                return ws[k, (s - 2) * batch_count + bb, r, :]

            signals = [
                piece(lambda s, r, bb=bb: xs[k, s * batch_count + bb, r, :]) for bb in range(batch_count)
            ]
            signals += [piece(lambda s, r, bb=bb: weighted_rows(s, r, bb)) for bb in range(batch_count)]
            signals.append(piece(lambda s, r: hs[k, s, r, :]))
            stacked = jnp.concatenate(signals, axis=1)
            grid = jnp.dot(enter_table[...], stacked, preferred_element_type=jnp.float32).astype(jnp.bfloat16)
            for i, (k1, part) in enumerate(live):
                at = i * ROWS
                spec[k1, pl.ds(pl.multiple_of(part * INNER + g * ROWS, ROWS), ROWS), :] = grid[at : at + ROWS]
            return inner

        lax.fori_loop(0, INNER // ROWS, enter, 0)

        def products(full):
            real, imag = full[:INNER], full[INNER:]

            def take(i):
                return real[:, i * LANES : (i + 1) * LANES], imag[:, i * LANES : (i + 1) * LANES]

            hr, hi = take(2 * batch_count)
            out_real, out_imag = [], []
            for bb in range(batch_count):
                mr, mi = take(bb)
                out_real.append(mr * hr - mi * hi)
                out_imag.append(mr * hi + mi * hr)
            for bb in range(batch_count):
                wr, wi = take(batch_count + bb)
                out_real.append(hr * wr + hi * wi)
                out_imag.append(hr * wi - hi * wr)
            slope_real, slope_imag = 0.0, 0.0
            for bb in range(batch_count):
                mr, mi = take(bb)
                wr, wi = take(batch_count + bb)
                slope_real = slope_real + (mr * wr + mi * wi)
                slope_imag = slope_imag + (mr * wi - mi * wr)
            out_real.append(slope_real)
            out_imag.append(slope_imag)
            return jnp.concatenate(
                [
                    jnp.concatenate([t.astype(jnp.bfloat16) for t in out_real], axis=1),
                    jnp.concatenate([t.astype(jnp.bfloat16) for t in out_imag], axis=1),
                ],
                axis=0,
            )

        def middle(firsts_now):
            fulls = [
                jnp.dot(middle_ref[scale * k1], spec[k1], preferred_element_type=jnp.float32) for k1 in firsts_now
            ]
            turned = [products(full) for full in fulls]
            backs = [
                jnp.dot(back_ref[scale * k1], turn, preferred_element_type=jnp.float32).astype(jnp.bfloat16)
                for k1, turn in zip(firsts_now, turned)
            ]
            for k1, back in zip(firsts_now, backs):
                spec[k1] = back

        def middle_pair(p, inner):
            middle([2 * p, 2 * p + 1])
            return inner

        lax.fori_loop(0, kept // 2, middle_pair, 0)
        middle([kept - 1])

        def leave(g, inner):
            stacked = jnp.concatenate(
                [
                    spec[k1, pl.ds(pl.multiple_of(part * INNER + g * ROWS, ROWS), ROWS), :]
                    for k1, part in live
                ],
                axis=0,
            )
            grid = jnp.dot(leave_table[...], stacked, preferred_element_type=jnp.float32).astype(jnp.bfloat16)
            for n1 in range(firsts):
                s = n1 // per_row
                r = pl.ds(pl.multiple_of(n1 % per_row * INNER + g * ROWS, ROWS), ROWS)
                part = grid[n1 * ROWS : (n1 + 1) * ROWS]
                for bb in range(batch_count):
                    if low:
                        ws[k, s * batch_count + bb, r, :] = part[:, bb * LANES : (bb + 1) * LANES]
                    elif s >= 2:
                        ws[k, (s - 2) * batch_count + bb, r, :] = part[:, bb * LANES : (bb + 1) * LANES]
                    at = batch_count + bb
                    to = s * batch_count + bb + (4 if low else 0)
                    xs[k, to, r, :] = part[:, at * LANES : (at + 1) * LANES]
                hs[k, s + (2 if low else 0), r, :] = part[:, 2 * batch_count * LANES :]
            return inner

        lax.fori_loop(0, INNER // ROWS, leave, 0)

    def merge_low(k):
        for zz in range(2):
            for bb in range(batch_count):
                at = zz * batch_count + bb
                arrived(cross.at[k, at], cross_recv.at[k, at])
                xs[k, 4 + at] = (
                    xs[k, 4 + at].astype(jnp.float32) + cross[k, at].astype(jnp.float32)
                ).astype(jnp.bfloat16)
            arrived(scross.at[k, zz], scross_recv.at[k, zz])
            hs[k, 2 + zz] = (
                hs[k, 2 + zz].astype(jnp.float32) + scross[k, zz].astype(jnp.float32)
            ).astype(jnp.bfloat16)
        give_low_corr(k, move)

    def finish_block(blk, carry):
        k = blk // batch_count
        pb = lax.rem(blk, batch_count)
        arrived(ys.at[blk], y_recv.at[blk])
        arrived(cs.at[blk], c_recv.at[blk])
        query = acts[0, blk].astype(jnp.float32)
        key = acts[1, blk].astype(jnp.float32)
        value = acts[2, blk].astype(jnp.float32)
        cot = acts[3, blk].astype(jnp.float32)
        skip = skip_ref[pl.ds(blk, 1), :]
        signal = ys[blk].astype(jnp.float32) + skip * stage[blk, 0].astype(jnp.float32)
        back = cs[blk].astype(jnp.float32) + skip * stage[blk, 1].astype(jnp.float32)
        acts[0, blk] = (query * signal).astype(jnp.bfloat16)
        acts[1, blk] = (cot * signal).astype(jnp.bfloat16)
        acts[2, blk] = (back * value).astype(jnp.bfloat16)
        acts[3, blk] = (back * key).astype(jnp.bfloat16)
        copies = output_copies(blk)
        for copy in copies[:4]:
            copy.start()
        arrived(ss.at[blk], s_recv.at[blk])

        @pl.when(pb == b)
        def _():
            remote(ss.at[blk], ss.at[blk], n_send.at[k], s_recv.at[blk], z, 1 - b).start()

        taps[blk] = factor * ss[blk].astype(jnp.float32)
        copies[4].start()
        return carry

    def finish_step(k):
        for bb in range(batch_count):
            finish_block(k * batch_count + lax.rem(b + bb, batch_count), 0)

    def finish_rest(m, carry):
        finish_step(merge_order(m))
        return carry

    lag = 5
    wait_upper = 4

    @pl.when(z == 0)
    def _():
        lax.fori_loop(0, steps, finish_rest, 0)

    @pl.when(z == 1)
    def _():
        def pass_on(k):
            for s in range(4):
                arrived(xs.at[k, s], x_recv.at[k, s])
            for s in range(2):
                arrived(hs.at[k, s], h_recv.at[k, s])
            forward_low(k, move)

            @pl.when(k < steps - ahead)
            def _():
                give_across(k + ahead, move)

        pass_on(0)

        def step(k, carry):
            @pl.when(k < steps - 1)
            def _():
                pass_on(k + 1)

            @pl.when(k < steps)
            def _():
                for s in range(4):
                    arrived(ws.at[k, s], w_recv.at[k, s])
                transform(k, True)
                give_low_conv(k, move)

            @pl.when(k >= lag)
            def _():
                merge_low(merge_order(k - lag))

            @pl.when(k >= lag + 1)
            def _():
                finish_step(merge_order(k - lag - 1))

            return carry

        lax.fori_loop(0, steps + lag, step, 0)
        finish_step(merge_order(steps - 1))

    @pl.when(z >= 2)
    def _():
        def step(k, carry):
            @pl.when(upper_owner(k) == z)
            def _():
                for s in range(8):
                    arrived(xs.at[k, s], x_recv.at[k, s])
                for s in range(4):
                    arrived(hs.at[k, s], h_recv.at[k, s])
                    arrived(ws.at[k, s], w_recv.at[k, s])
                transform(k, False)
                give_upper(k, move)

            @pl.when(k >= wait_upper)
            def _():
                finish_step(merge_order(k - wait_upper))

            return carry

        lax.fori_loop(0, steps, step, 0)

        def rest(m, carry):
            finish_step(merge_order(m))
            return carry

        lax.fori_loop(steps - wait_upper, steps, rest, 0)

    def wait_gain(i, carry):
        _, _, idx = partner(i)
        arrived(gain.at[idx], g_recv.at[idx])
        arrived(gain.at[me], g_send.at[idx])
        return carry

    lax.fori_loop(0, groups - 1, wait_gain, 0)
    total = gain[0]
    for s in range(1, groups):
        total = total + gain[s]
    gs_ref[...] = factor * total

    def drain(blk, carry):
        for copy in output_copies(blk):
            copy.wait()
        give_inputs(blk, settle)
        k = blk // batch_count

        @pl.when(lax.rem(blk, batch_count) == b)
        def _():
            arrived(ss.at[blk], n_send.at[k])

            @pl.when(z == 1)
            def _():
                give_across(k, settle)
                forward_low(k, settle)
                give_low_conv(k, settle)
                give_low_corr(k, settle)

            @pl.when(upper_owner(k) == z)
            def _():
                give_upper(k, settle)

        return carry

    lax.fori_loop(0, block_count, drain, 0)


def fused(query_proj, key_proj, value_proj, cotangent, long_filter, skip_gain):
    rows, width = query_proj.shape[1:]
    seq_count = lax.axis_size("seq")
    batch_count = lax.axis_size("dp")
    groups = seq_count * batch_count
    seq_length = seq_count * rows
    block_count = width // LANES
    steps = block_count // batch_count
    factor = (batch_count * seq_length) ** (-0.5)
    tables = transform_tables(seq_length)
    low_tables = transform_tables(seq_length // 2)
    tables = tables + (low_tables[0], low_tables[3])
    kept = tables[1].shape[0]
    signals = 2 * batch_count + 1
    half = jnp.bfloat16
    dma = pltpu.SemaphoreType.DMA
    hbm = pl.BlockSpec(memory_space=pl.ANY)
    vmem = pl.BlockSpec(memory_space=pltpu.VMEM)
    flops = 2 * steps * signals * LANES * (2 * tables[0].size * INNER // ROWS + 2 * tables[1].size)
    results = pl.pallas_call(
        functools.partial(fused_kernel, factor),
        out_shape=[jax.ShapeDtypeStruct((1, rows, width), half)] * 4
        + [
            jax.ShapeDtypeStruct((rows, width), jnp.float32),
            jax.ShapeDtypeStruct((block_count, LANES), jnp.float32),
        ],
        in_specs=[hbm] * 5 + [vmem] * 7,
        out_specs=[hbm] * 5 + [vmem],
        scratch_shapes=[
            pltpu.VMEM((4, block_count, rows, LANES), half),
            pltpu.VMEM((block_count, rows, LANES), jnp.float32),
            pltpu.VMEM((block_count, 2, rows, LANES), half),
            pltpu.VMEM((steps, rows, LANES), half),
            pltpu.VMEM((steps, groups, rows, LANES), half),
            pltpu.VMEM((steps, groups // 2, rows, LANES), half),
            pltpu.VMEM((steps, seq_count, rows, LANES), half),
            pltpu.VMEM((steps, groups // 2, rows, LANES), half),
            pltpu.VMEM((steps, seq_count // 2, rows, LANES), half),
            pltpu.VMEM((kept, 2 * INNER, signals * LANES), half),
            pltpu.VMEM((block_count, rows, LANES), half),
            pltpu.VMEM((block_count, rows, LANES), half),
            pltpu.VMEM((block_count, rows, LANES), half),
            pltpu.VMEM((groups, block_count, LANES), jnp.float32),
            dma((5, block_count)),
            dma((5, block_count)),
            dma((block_count,)),
            dma((block_count,)),
            dma((block_count,)),
            dma((steps,)),
            dma((steps,)),
            dma((steps, 3)),
            dma((steps, groups // 2)),
            dma((steps, groups)),
            dma((steps, seq_count)),
            dma((steps,)),
            dma((groups,)),
            dma((steps, groups)),
            dma((steps, groups // 2)),
            dma((steps, seq_count)),
            dma((steps, groups // 2)),
            dma((steps, seq_count // 2)),
            dma((block_count,)),
            dma((block_count,)),
            dma((block_count,)),
            dma((groups,)),
        ],
        compiler_params=pltpu.CompilerParams(
            collective_id=0, has_side_effects=True, vmem_limit_bytes=62 * 1024 * 1024
        ),
        cost_estimate=pl.CostEstimate(
            flops=flops, bytes_accessed=24 * rows * width, transcendentals=0
        ),
    )(
        query_proj, key_proj, value_proj, cotangent, long_filter,
        skip_gain.reshape(block_count, LANES), *(jnp.asarray(t) for t in tables),
    )
    return tuple(results[:5]) + (results[5].reshape(width),)


def dft_tables(seq_length):
    full_size = 2 * seq_length
    inner_size = 128
    outer_size = full_size // inner_size
    half_size = outer_size // 2
    outer_index = jnp.arange(outer_size, dtype=jnp.int32)
    half_index = jnp.arange(half_size, dtype=jnp.int32)
    inner_index = jnp.arange(inner_size, dtype=jnp.int32)
    first_angle = (
        2.0
        * math.pi
        / outer_size
        * (outer_index[:, None] * half_index[None, :] % outer_size).astype(jnp.float32)
    )
    twist_angle = (
        2.0
        * math.pi
        / full_size
        * (outer_index[:, None] * inner_index[None, :] % full_size).astype(jnp.float32)
    )
    last_angle = (
        2.0
        * math.pi
        / inner_size
        * (inner_index[:, None] * inner_index[None, :] % inner_size).astype(jnp.float32)
    )
    return (
        jnp.cos(first_angle),
        jnp.sin(first_angle),
        jnp.cos(twist_angle),
        jnp.sin(twist_angle),
        jnp.cos(last_angle),
        jnp.sin(last_angle),
    )


def forward(signal, tables):
    cos_first, sin_first, cos_twist, sin_twist, cos_last, sin_last = tables
    half_size = cos_first.shape[1]
    signal_grid = signal.reshape(signal.shape[0], half_size, 128)
    real_first = jnp.einsum("kn,rnm->rkm", cos_first, signal_grid, precision=full_precision)
    imag_first = -jnp.einsum("kn,rnm->rkm", sin_first, signal_grid, precision=full_precision)
    real_twist = real_first * cos_twist + imag_first * sin_twist
    imag_twist = imag_first * cos_twist - real_first * sin_twist
    real_last = jnp.einsum(
        "rkm,mj->rkj", real_twist, cos_last, precision=full_precision
    ) + jnp.einsum("rkm,mj->rkj", imag_twist, sin_last, precision=full_precision)
    imag_last = jnp.einsum(
        "rkm,mj->rkj", imag_twist, cos_last, precision=full_precision
    ) - jnp.einsum("rkm,mj->rkj", real_twist, sin_last, precision=full_precision)
    return (real_last, imag_last)


def inverse(real_part, imag_part, tables):
    cos_first, sin_first, cos_twist, sin_twist, cos_last, sin_last = tables
    half_size = cos_first.shape[1]
    row_total = real_part.shape[0]
    real_inner = jnp.einsum(
        "rkj,jm->rkm", real_part, cos_last, precision=full_precision
    ) - jnp.einsum("rkj,jm->rkm", imag_part, sin_last, precision=full_precision)
    imag_inner = jnp.einsum(
        "rkj,jm->rkm", imag_part, cos_last, precision=full_precision
    ) + jnp.einsum("rkj,jm->rkm", real_part, sin_last, precision=full_precision)
    real_twist = real_inner * cos_twist - imag_inner * sin_twist
    imag_twist = imag_inner * cos_twist + real_inner * sin_twist
    result = jnp.einsum(
        "kn,rkm->rnm", cos_first, real_twist, precision=full_precision
    ) - jnp.einsum("kn,rkm->rnm", sin_first, imag_twist, precision=full_precision)
    return (result / (2.0 * half_size * 128)).reshape(row_total, half_size * 128)


def filter_block(items, tables):
    mixed_blk, weighted_blk, kernel = items
    batches, chan_width, seq_length = mixed_blk.shape
    row_count = batches * chan_width
    mixed_wide = mixed_blk.astype(jnp.float32)
    weighted_wide = weighted_blk.astype(jnp.float32)
    stacked = jnp.concatenate(
        [
            mixed_wide.reshape(row_count, seq_length),
            weighted_wide.reshape(row_count, seq_length),
            kernel,
        ],
        axis=0,
    )
    real_spec, imag_spec = forward(stacked, tables)
    grid_shape = real_spec.shape[1:]
    mixed_real = real_spec[:row_count].reshape((batches, chan_width) + grid_shape)
    mixed_imag = imag_spec[:row_count].reshape((batches, chan_width) + grid_shape)
    weighted_real = real_spec[row_count : 2 * row_count].reshape((batches, chan_width) + grid_shape)
    weighted_imag = imag_spec[row_count : 2 * row_count].reshape((batches, chan_width) + grid_shape)
    kernel_real = real_spec[2 * row_count :][None]
    kernel_imag = imag_spec[2 * row_count :][None]
    conv_real = mixed_real * kernel_real - mixed_imag * kernel_imag
    conv_imag = mixed_real * kernel_imag + mixed_imag * kernel_real
    corr_real = kernel_real * weighted_real + kernel_imag * weighted_imag
    corr_imag = kernel_real * weighted_imag - kernel_imag * weighted_real
    slope_real = jnp.sum(mixed_real * weighted_real + mixed_imag * weighted_imag, axis=0)
    slope_imag = jnp.sum(mixed_real * weighted_imag - mixed_imag * weighted_real, axis=0)
    spec_real = jnp.concatenate(
        [
            conv_real.reshape((row_count,) + grid_shape),
            corr_real.reshape((row_count,) + grid_shape),
            slope_real,
        ],
        axis=0,
    )
    spec_imag = jnp.concatenate(
        [
            conv_imag.reshape((row_count,) + grid_shape),
            corr_imag.reshape((row_count,) + grid_shape),
            slope_imag,
        ],
        axis=0,
    )
    result = inverse(spec_real, spec_imag, tables)
    conv_vals = result[:row_count].reshape(batches, chan_width, seq_length).astype(jnp.bfloat16)
    corr_vals = (
        result[row_count : 2 * row_count]
        .reshape(batches, chan_width, seq_length)
        .astype(jnp.bfloat16)
    )
    slope = result[2 * row_count :]
    return (conv_vals, corr_vals, slope)


def run_blocks(mixed_rows, weighted_rows, filter_part):
    batches, part_width, seq_length = mixed_rows.shape
    block_width = min(part_width, 8)
    block_count = part_width // block_width
    tables = dft_tables(seq_length)

    def stack_rows(arr):
        return jnp.moveaxis(arr.reshape(batches, block_count, block_width, seq_length), 1, 0)

    def unstack_rows(arr):
        return jnp.moveaxis(arr, 0, 1).reshape(batches, part_width, seq_length)

    def one_block(items):
        return filter_block(items, tables)

    items = (
        stack_rows(mixed_rows),
        stack_rows(weighted_rows),
        filter_part.reshape(block_count, block_width, seq_length),
    )
    conv_vals, corr_vals, slope = lax.map(one_block, items)
    return (unstack_rows(conv_vals), unstack_rows(corr_vals), slope.reshape(part_width, seq_length))


def on_device(query_proj, key_proj, value_proj, cotangent, long_filter, skip_gain):
    rows, width = query_proj.shape[1:]
    grouped = lax.axis_size("seq") == 4 and lax.axis_size("dp") == 2
    if grouped and rows % INNER == 0 and width >= 16 * LANES and width % (2 * LANES) == 0 and rows * width <= 2**20:
        return fused(query_proj, key_proj, value_proj, cotangent, long_filter, skip_gain)
    return spread(query_proj, key_proj, value_proj, cotangent, long_filter, skip_gain)


def spread(query_proj, key_proj, value_proj, cotangent, long_filter, skip_gain):
    query_rows = query_proj[0].astype(jnp.float32)
    key_rows = key_proj[0].astype(jnp.float32)
    value_rows = value_proj[0].astype(jnp.float32)
    cot_rows = cotangent[0].astype(jnp.float32)
    local_length = query_proj.shape[1]
    chan_width = query_proj.shape[2]
    seq_count = lax.axis_size("seq")
    batch_count = lax.axis_size("dp")
    factor = (batch_count * seq_count * local_length) ** (-0.5)
    mixed = (key_rows * value_rows).astype(jnp.bfloat16)
    weighted = (cot_rows * query_rows).astype(jnp.bfloat16)
    mixed_wide = mixed.astype(jnp.float32)
    weighted_wide = weighted.astype(jnp.float32)
    gain_term = factor * jnp.sum(weighted_wide * mixed_wide, axis=0)
    grad_skip = lax.psum(gain_term, ("seq", "dp"))
    filter_share = lax.all_to_all(long_filter.T, "seq", split_axis=0, concat_axis=1, tiled=True)
    groups = seq_count * batch_count
    share_width = chan_width // groups
    mixed_cols, weighted_cols = (
        lax.all_to_all(mixed.T, ("seq", "dp"), split_axis=0, concat_axis=1, tiled=True),
        lax.all_to_all(weighted.T, ("seq", "dp"), split_axis=0, concat_axis=1, tiled=True),
    )

    def to_sequences(arr):
        arr = arr.reshape(share_width, seq_count, batch_count, local_length)
        return jnp.transpose(arr, (2, 0, 1, 3)).reshape(
            batch_count, share_width, seq_count * local_length
        )

    def to_pieces(arr):
        arr = arr.reshape(batch_count, share_width, seq_count, local_length)
        return jnp.transpose(arr, (1, 2, 0, 3)).reshape(share_width, groups * local_length)

    filter_part = lax.dynamic_slice_in_dim(
        filter_share, lax.axis_index("dp") * share_width, share_width, 0
    )
    conv_vals, corr_vals, slope = run_blocks(
        to_sequences(mixed_cols), to_sequences(weighted_cols), filter_part
    )
    conv_back, corr_back = (
        lax.all_to_all(
            to_pieces(conv_vals), ("seq", "dp"), split_axis=1, concat_axis=0, tiled=True
        ),
        lax.all_to_all(
            to_pieces(corr_vals), ("seq", "dp"), split_axis=1, concat_axis=0, tiled=True
        ),
    )
    slope_share = lax.all_gather(slope, "dp", axis=0, tiled=True)
    slope_rows = lax.all_to_all(slope_share, "seq", split_axis=1, concat_axis=0, tiled=True)
    grad_filter = factor * slope_rows.T
    conv_rows = conv_back.T.astype(jnp.float32)
    corr_rows = corr_back.T.astype(jnp.float32)
    signal = conv_rows + skip_gain[None, :] * mixed_wide
    output = (query_rows * signal).astype(jnp.bfloat16)
    grad_query = (cot_rows * signal).astype(jnp.bfloat16)
    back = corr_rows + skip_gain[None, :] * weighted_wide
    grad_key = (back * value_rows).astype(jnp.bfloat16)
    grad_value = (back * key_rows).astype(jnp.bfloat16)
    return (
        output[None],
        grad_query[None],
        grad_key[None],
        grad_value[None],
        grad_filter,
        grad_skip,
    )


def solution(mesh):
    return jax.shard_map(
        on_device,
        mesh=mesh,
        in_specs=(
            P("dp", "seq", "chan"),
            P("dp", "seq", "chan"),
            P("dp", "seq", "chan"),
            P("dp", "seq", "chan"),
            P("seq", "chan"),
            P("chan"),
        ),
        out_specs=(
            P("dp", "seq", "chan"),
            P("dp", "seq", "chan"),
            P("dp", "seq", "chan"),
            P("dp", "seq", "chan"),
            P("seq", "chan"),
            P("chan"),
        ),
        check_vma=False,
    )
```
